32 devices in a mesh: grp: 2 (over y), exp: 16 (over z, x, core).
Axes of the slice: x: 2, y: 2, z: 4, core: 2. Of those that a mesh axis runs over, the one named last changes fastest.
Arguments:
- output_gradient: bfloat16 [512, 2048], P(('grp', 'exp')), parts along dimension 0, may hold values from -6 to 6
- input_tokens: bfloat16 [512, 2048], P(('grp', 'exp')), parts along dimension 0, may hold values from -6 to 6
- routes: int32 [512, 8], P(('grp', 'exp')), parts along dimension 0, may hold values from 0 to 15, all different within a row; in each aligned block of 16 rows (0 to 15, 16 to 31, ...) at most 16 rows name the same one
- combine: bfloat16 [512, 8], P(('grp', 'exp')), parts along dimension 0, may hold values from 0.019897461 to 0.5
- gate_matrix: bfloat16 [16, 2048, 768], P('exp'), may hold values from -0.125 to 0.125
- upward_matrix: bfloat16 [16, 2048, 768], P('exp'), may hold values from -0.125 to 0.125
- down_matrix: bfloat16 [16, 768, 2048], P('exp'), may hold values from -0.21875 to 0.21875
- gate_adapter_left: bfloat16 [2048, 16], replicated, may hold values from -0.125 to 0.125
- gate_adapter_right: bfloat16 [16, 768], replicated, may hold values from -0.375 to 0.375
- upward_adapter_left: bfloat16 [2048, 16], replicated, may hold values from -0.125 to 0.125
- upward_adapter_right: bfloat16 [16, 768], replicated, may hold values from -0.375 to 0.375
- down_adapter_left: bfloat16 [768, 16], replicated, may hold values from -0.21875 to 0.21875
- down_adapter_right: bfloat16 [16, 2048], replicated, may hold values from -0.375 to 0.375
Outputs:
- grad_in: bfloat16 [512, 2048], P(('grp', 'exp')), parts along dimension 0
- grad_combine: bfloat16 [512, 8], P(('grp', 'exp')), parts along dimension 0
- grad_adapters: float32 [270336], P(('grp', 'exp')), parts along dimension 0
The draws below stay inside these ranges and needn't reach their ends.
There are 2 independent parts, one for each index of `grp`. The reference program is written for one: setup_inputs(seed, part) draws one part's arguments, and reference() takes and returns one part's arrays. A program takes and returns all parts, laid end to end along the dimension named above; an argument that names none is the same for every part. Nothing has to cross between parts.
Inputs may be any that keep to these rules, and one draw needn't show every extreme that they name: `routes`: within each aligned block of 16 rows (the tokens of one device) no expert is named more than 16 times; in every draw some block names some expert exactly 16 times. A row names 8 different experts.
All inputs are finite; a program needn't handle non-finite values.
Results may differ from the reference program's by a relative error of at most 0.0085.
Values may be sent and summed in bfloat16 or wider, within the bound.
A program may use at most 64 MiB of HBM per device.

```python
import math
import jax
import jax.numpy as jnp
import numpy as np
from jax import lax

MODEL_DIMENSION = 2048
EXPERT_HIDDEN = 768
ADAPTER_RANK = 16
TOP = 8
TOK_DEV = 16
EXPERTS = 16
TOKENS = 256
CAP = 16
PARAMS = 135168
N_EXP = 16


def block_levels(key, shape, shards, smallest, largest):
    def one(dim, shards_of):
        draws = jax.random.uniform(jax.random.fold_in(jax.random.fold_in(key, 6), dim), (shards_of,), jnp.float32, smallest / len(shards), largest / len(shards))
        return jnp.repeat(jnp.exp(draws), shape[dim] // shards_of).reshape((-1,) + (1,) * (len(shape) - dim - 1))

    loudness = one(*shards[0])
    for cut in shards[1:]:
        loudness = loudness * one(*cut)
    return loudness


def assign_block(rng, own, number, rows, amount, top, most, slope):
    ranking = jax.random.permutation(rng, amount)
    packed, ordinary = load_shares(amount, rows * top, most, slope, True), load_shares(amount, rows * top, most, slope, False)
    places = jnp.arange(amount)

    def named(tallies, rotation):
        used = int((tallies > 0).sum())
        fixed = max(1, used // 4)
        passed = fixed + (places - fixed + rotation * (used - fixed)) % max(1, amount - fixed)
        return jnp.zeros((amount,), jnp.int32).at[ranking[jnp.where(places < fixed, places, passed)]].set(jnp.asarray(tallies, jnp.int32))

    tallies = jnp.where(number % 4 == 0, named(packed, number // 4), named(ordinary, number - number // 4 - 1))
    mixed = jax.random.permutation(jax.random.fold_in(own, 3), amount)
    donor, receiver = mixed[0:amount // 2 * 2:2], mixed[1:amount // 2 * 2:2]
    margin = jnp.minimum(tallies[donor] - 1, most - tallies[receiver]) // 2
    margin = jnp.where((donor == ranking[0]) | (receiver == ranking[0]) | (tallies[receiver] == 0), 0, jnp.maximum(margin, 0))
    passed = jax.random.randint(jax.random.fold_in(own, 4), (amount // 2,), 0, 1 << 20) % (margin + 1)
    tallies = tallies.at[donor].add(-passed).at[receiver].add(passed)
    items = jnp.searchsorted(jnp.cumsum(tallies), jnp.arange(rows * top), side="right").astype(jnp.int32)
    listing = items.reshape(top, rows).T
    listing = listing[jax.random.permutation(jax.random.fold_in(own, 1), rows)]
    rotation = jax.random.randint(jax.random.fold_in(own, 2), (rows, 1), 0, top)
    return jnp.take_along_axis(listing, (jnp.arange(top)[None, :] + rotation) % top, axis=1)


def load_shares(count, total, limit, slope, full):
    portions = [(1 << 20) // math.isqrt(rank ** slope) + 1 for rank in range(1, count + 1)]
    largest = limit if full else min(limit, max(-(-total // count), total * portions[0] // sum(portions)))
    least = 1 if total - largest >= count - 1 else 0
    counts, rest = [largest] + [least] * (count - 1), total - largest - least * (count - 1)
    while rest > 0:
        free = [i for i in range(1, count) if counts[i] < largest] or [i for i in range(1, count) if counts[i] < limit]
        mass, budget = sum([portions[i] for i in free]), rest
        for i in free:
            more = min(limit - counts[i], max(1, budget * portions[i] // mass), rest)
            counts[i] = counts[i] + more
            rest = rest - more
    return np.array(counts)


def gaussian(stream_key, dims, deviation, most, cuts=(), held_as=jnp.bfloat16):
    result = deviation * jax.random.normal(stream_key, dims, jnp.float32)
    if cuts:
        result = result * block_levels(stream_key, dims, cuts, -0.22, 0.18)
    return jnp.clip(result, -most, most).astype(held_as)


def setup_inputs(seed: int = 0, part: int = 0) -> dict:
    key_of = jax.random.split(jax.random.key(seed), 14)
    part_splits = jax.random.split(jax.random.fold_in(key_of[13], part), 14)
    output_gradient = gaussian(part_splits[0], (TOKENS, MODEL_DIMENSION), 1.0, 6.0, ((0, 16),))
    input_tokens = gaussian(part_splits[1], (TOKENS, MODEL_DIMENSION), 1.0, 6.0, ((0, 16),))
    routes_keys = jax.random.split(jax.random.fold_in(part_splits[2], 1), TOKENS // TOK_DEV)
    routes_turns = jax.random.permutation(jax.random.fold_in(part_splits[2], 3), TOKENS // TOK_DEV)
    routes = jax.vmap(lambda own, number: assign_block(jax.random.fold_in(part_splits[2], 2), own, number, TOK_DEV, EXPERTS, TOP, CAP, 2))(routes_keys, routes_turns).reshape((TOKENS, TOP))
    combine = jnp.clip(jnp.exp(math.log(0.5) - 3.224016 * jax.random.uniform(part_splits[3], (TOKENS, TOP), jnp.float32) ** block_levels(part_splits[3], (TOKENS, TOP), ((0, 16),), -0.2, 0.2)), 0.019897461, 0.5).astype(jnp.bfloat16)
    gate_matrix = gaussian(key_of[4], (EXPERTS, MODEL_DIMENSION, EXPERT_HIDDEN), MODEL_DIMENSION ** -0.5, 0.125, ((0, 16),))
    upward_matrix = gaussian(key_of[5], (EXPERTS, MODEL_DIMENSION, EXPERT_HIDDEN), MODEL_DIMENSION ** -0.5, 0.125, ((0, 16),))
    down_matrix = gaussian(key_of[6], (EXPERTS, EXPERT_HIDDEN, MODEL_DIMENSION), EXPERT_HIDDEN ** -0.5, 0.21875, ((0, 16),))
    gate_adapter_left = gaussian(key_of[7], (MODEL_DIMENSION, ADAPTER_RANK), MODEL_DIMENSION ** -0.5, 0.125)
    gate_adapter_right = gaussian(key_of[8], (ADAPTER_RANK, EXPERT_HIDDEN), 0.0625, 0.375)
    upward_adapter_left = gaussian(key_of[9], (MODEL_DIMENSION, ADAPTER_RANK), MODEL_DIMENSION ** -0.5, 0.125)
    upward_adapter_right = gaussian(key_of[10], (ADAPTER_RANK, EXPERT_HIDDEN), 0.0625, 0.375)
    down_adapter_left = gaussian(key_of[11], (EXPERT_HIDDEN, ADAPTER_RANK), EXPERT_HIDDEN ** -0.5, 0.21875)
    down_adapter_right = gaussian(key_of[12], (ADAPTER_RANK, MODEL_DIMENSION), 0.0625, 0.375)
    return dict(output_gradient=output_gradient, input_tokens=input_tokens, routes=routes, combine=combine, gate_matrix=gate_matrix, upward_matrix=upward_matrix, down_matrix=down_matrix, gate_adapter_left=gate_adapter_left, gate_adapter_right=gate_adapter_right, upward_adapter_left=upward_adapter_left, upward_adapter_right=upward_adapter_right, down_adapter_left=down_adapter_left, down_adapter_right=down_adapter_right)


adapter_scale = 2.0


def expert_forward_pass(incoming_rows, gate_matrix, upward_matrix, gate_adapter_left, gate_adapter_right, upward_adapter_left, upward_adapter_right, down_adapter_left):
    lowrank_gate = jnp.dot(incoming_rows, gate_adapter_left, preferred_element_type=jnp.float32).astype(jnp.bfloat16)
    lowrank_upward = jnp.dot(incoming_rows, upward_adapter_left, preferred_element_type=jnp.float32).astype(jnp.bfloat16)
    gate_preactivation = jnp.dot(incoming_rows, gate_matrix, preferred_element_type=jnp.float32) + adapter_scale * jnp.dot(lowrank_gate, gate_adapter_right, preferred_element_type=jnp.float32)
    upward_preactivation = jnp.dot(incoming_rows, upward_matrix, preferred_element_type=jnp.float32) + adapter_scale * jnp.dot(lowrank_upward, upward_adapter_right, preferred_element_type=jnp.float32)
    hidden_activation = (jax.nn.silu(gate_preactivation) * upward_preactivation).astype(jnp.bfloat16)
    lowrank_hidden = jnp.dot(hidden_activation, down_adapter_left, preferred_element_type=jnp.float32).astype(jnp.bfloat16)
    return (lowrank_gate, lowrank_upward, gate_preactivation, upward_preactivation, hidden_activation, lowrank_hidden)


def expert_reverse_pass(saved_activations, incoming_rows, gradient_rows, gate_row_values, gate_matrix, upward_matrix, down_matrix, gate_adapter_left, gate_adapter_right, upward_adapter_left, upward_adapter_right, down_adapter_left, down_adapter_right):
    lowrank_gate, lowrank_upward, gate_preactivation, upward_preactivation, hidden_activation, lowrank_hidden = saved_activations
    backward_lowrank = jnp.dot(gradient_rows, down_adapter_right.T, preferred_element_type=jnp.float32)
    backward_truncated = backward_lowrank.astype(jnp.bfloat16)
    hidden_unscaled = jnp.dot(gradient_rows, down_matrix.T, preferred_element_type=jnp.float32) + adapter_scale * jnp.dot(backward_truncated, down_adapter_left.T, preferred_element_type=jnp.float32)
    weight_row_values = jnp.sum(hidden_activation.astype(jnp.float32) * hidden_unscaled, axis=1).astype(jnp.bfloat16)
    scales = gate_row_values.astype(jnp.float32)[:, None]
    hidden_grad = scales * hidden_unscaled
    logistic = jax.nn.sigmoid(gate_preactivation)
    gate_gradient = (hidden_grad * upward_preactivation * logistic * (1.0 + gate_preactivation * (1.0 - logistic))).astype(jnp.bfloat16)
    upward_gradient = (hidden_grad * gate_preactivation * logistic).astype(jnp.bfloat16)
    gate_reverse = jnp.dot(gate_gradient, gate_adapter_right.T, preferred_element_type=jnp.float32).astype(jnp.bfloat16)
    upward_reverse = jnp.dot(upward_gradient, upward_adapter_right.T, preferred_element_type=jnp.float32).astype(jnp.bfloat16)
    input_row_values = jnp.dot(gate_gradient, gate_matrix.T, preferred_element_type=jnp.float32) + jnp.dot(upward_gradient, upward_matrix.T, preferred_element_type=jnp.float32)
    input_row_values = input_row_values + adapter_scale * (jnp.dot(gate_reverse, gate_adapter_left.T, preferred_element_type=jnp.float32) + jnp.dot(upward_reverse, upward_adapter_left.T, preferred_element_type=jnp.float32))
    input_row_values = input_row_values.astype(jnp.bfloat16)
    scaled_rows = (scales * gradient_rows.astype(jnp.float32)).astype(jnp.bfloat16)
    scaled_low = (scales * backward_lowrank).astype(jnp.bfloat16)
    partial_results = [
        jnp.dot(incoming_rows.T, gate_reverse, preferred_element_type=jnp.float32),
        jnp.dot(lowrank_gate.T, gate_gradient, preferred_element_type=jnp.float32),
        jnp.dot(incoming_rows.T, upward_reverse, preferred_element_type=jnp.float32),
        jnp.dot(lowrank_upward.T, upward_gradient, preferred_element_type=jnp.float32),
        jnp.dot(hidden_activation.T, scaled_low, preferred_element_type=jnp.float32),
        jnp.dot(lowrank_hidden.T, scaled_rows, preferred_element_type=jnp.float32),
    ]
    adapter_products = adapter_scale * jnp.concatenate([partial_result.reshape(-1) for partial_result in partial_results])
    return input_row_values, weight_row_values, adapter_products


def reference(output_gradient, input_tokens, routes, combine, gate_matrix, upward_matrix, down_matrix, gate_adapter_left, gate_adapter_right, upward_adapter_left, upward_adapter_right, down_adapter_left, down_adapter_right):
    pick_count = TOKENS * TOP
    blocked = routes.reshape(N_EXP, TOK_DEV * TOP)
    onehot = (blocked[:, :, None] == jnp.arange(EXPERTS, dtype=jnp.int32)[None, None, :]).astype(jnp.int32)
    earlier = jnp.cumsum(onehot, axis=1) - onehot
    position = jnp.sum(earlier * onehot, axis=2)
    source = jnp.arange(N_EXP, dtype=jnp.int32)[:, None]
    placed = (blocked * (N_EXP * CAP) + source * CAP + position).reshape(-1).astype(jnp.int32)
    inverse = jnp.full((EXPERTS * N_EXP * CAP,), pick_count, jnp.int32)
    inverse = inverse.at[placed].set(jnp.arange(pick_count, dtype=jnp.int32)).reshape(EXPERTS, N_EXP * CAP)
    inputs_ext = jnp.concatenate([input_tokens, jnp.zeros((1, MODEL_DIMENSION), input_tokens.dtype)], axis=0)
    grads_ext = jnp.concatenate([output_gradient, jnp.zeros((1, MODEL_DIMENSION), output_gradient.dtype)], axis=0)
    weights_ext = jnp.concatenate([combine.reshape(-1), jnp.zeros((1,), combine.dtype)], axis=0)

    def one_expert(carried, expert_index):
        input_sums, weight_table, adapter_sums = carried
        members = inverse[expert_index]
        owners = (members // TOP).astype(jnp.int32)
        incoming_rows = inputs_ext[owners]
        gradient_rows = grads_ext[owners]
        gate_row_values = weights_ext[members]
        saved_activations = expert_forward_pass(incoming_rows, gate_matrix[expert_index], upward_matrix[expert_index], gate_adapter_left, gate_adapter_right, upward_adapter_left, upward_adapter_right, down_adapter_left)
        input_row_values, weight_row_values, adapter_products = expert_reverse_pass(saved_activations, incoming_rows, gradient_rows, gate_row_values, gate_matrix[expert_index], upward_matrix[expert_index], down_matrix[expert_index], gate_adapter_left, gate_adapter_right, upward_adapter_left, upward_adapter_right, down_adapter_left, down_adapter_right)
        input_sums = input_sums.at[owners].add(input_row_values.astype(jnp.float32))
        weight_table = weight_table.at[members].set(weight_row_values)
        return (input_sums, weight_table, adapter_sums + adapter_products), None

    starting = (jnp.zeros((TOKENS + 1, MODEL_DIMENSION), jnp.float32), jnp.zeros((pick_count + 1,), jnp.bfloat16), jnp.zeros((PARAMS,), jnp.float32))
    (input_sums, weight_table, adapter_sums), _ = lax.scan(one_expert, starting, jnp.arange(EXPERTS, dtype=jnp.int32))
    grad_in = input_sums[:TOKENS].astype(jnp.bfloat16)
    grad_combine = weight_table[:pick_count].reshape(TOKENS, TOP)
    return grad_in, grad_combine, adapter_sums
```

```python
import functools

import jax
import jax.numpy as jnp
from jax import lax
from jax.experimental import pallas as pl
from jax.experimental.pallas import tpu as pltpu
from jax.sharding import PartitionSpec as P

adapter_scale = 2.0


def expert_forward_pass(
    incoming_rows,
    gate_matrix,
    upward_matrix,
    gate_adapter_left,
    gate_adapter_right,
    upward_adapter_left,
    upward_adapter_right,
    down_adapter_left,
):
    lowrank_gate = jnp.dot(
        incoming_rows, gate_adapter_left, preferred_element_type=jnp.float32
    ).astype(jnp.bfloat16)
    lowrank_upward = jnp.dot(
        incoming_rows, upward_adapter_left, preferred_element_type=jnp.float32
    ).astype(jnp.bfloat16)
    gate_preactivation = jnp.dot(
        incoming_rows, gate_matrix, preferred_element_type=jnp.float32
    ) + adapter_scale * jnp.dot(
        lowrank_gate, gate_adapter_right, preferred_element_type=jnp.float32
    )
    upward_preactivation = jnp.dot(
        incoming_rows, upward_matrix, preferred_element_type=jnp.float32
    ) + adapter_scale * jnp.dot(
        lowrank_upward, upward_adapter_right, preferred_element_type=jnp.float32
    )
    hidden_activation = (jax.nn.silu(gate_preactivation) * upward_preactivation).astype(
        jnp.bfloat16
    )
    lowrank_hidden = jnp.dot(
        hidden_activation, down_adapter_left, preferred_element_type=jnp.float32
    ).astype(jnp.bfloat16)
    return (
        lowrank_gate,
        lowrank_upward,
        gate_preactivation,
        upward_preactivation,
        hidden_activation,
        lowrank_hidden,
    )


def expert_reverse_pass(
    saved_activations,
    incoming_rows,
    gradient_rows,
    gate_row_values,
    gate_matrix,
    upward_matrix,
    down_matrix,
    gate_adapter_left,
    gate_adapter_right,
    upward_adapter_left,
    upward_adapter_right,
    down_adapter_left,
    down_adapter_right,
):
    (
        lowrank_gate,
        lowrank_upward,
        gate_preactivation,
        upward_preactivation,
        hidden_activation,
        lowrank_hidden,
    ) = saved_activations
    backward_lowrank = jnp.dot(
        gradient_rows, down_adapter_right.T, preferred_element_type=jnp.float32
    )
    backward_truncated = backward_lowrank.astype(jnp.bfloat16)
    hidden_unscaled = jnp.dot(
        gradient_rows, down_matrix.T, preferred_element_type=jnp.float32
    ) + adapter_scale * jnp.dot(
        backward_truncated, down_adapter_left.T, preferred_element_type=jnp.float32
    )
    weight_row_values = jnp.sum(
        hidden_activation.astype(jnp.float32) * hidden_unscaled, axis=1
    ).astype(jnp.bfloat16)
    scales = gate_row_values.astype(jnp.float32)[:, None]
    hidden_grad = scales * hidden_unscaled
    logistic = jax.nn.sigmoid(gate_preactivation)
    gate_gradient = (
        hidden_grad
        * upward_preactivation
        * logistic
        * (1.0 + gate_preactivation * (1.0 - logistic))
    ).astype(jnp.bfloat16)
    upward_gradient = (hidden_grad * gate_preactivation * logistic).astype(jnp.bfloat16)
    gate_reverse = jnp.dot(
        gate_gradient, gate_adapter_right.T, preferred_element_type=jnp.float32
    ).astype(jnp.bfloat16)
    upward_reverse = jnp.dot(
        upward_gradient, upward_adapter_right.T, preferred_element_type=jnp.float32
    ).astype(jnp.bfloat16)
    input_row_values = jnp.dot(
        gate_gradient, gate_matrix.T, preferred_element_type=jnp.float32
    ) + jnp.dot(upward_gradient, upward_matrix.T, preferred_element_type=jnp.float32)
    input_row_values = input_row_values + adapter_scale * (
        jnp.dot(gate_reverse, gate_adapter_left.T, preferred_element_type=jnp.float32)
        + jnp.dot(upward_reverse, upward_adapter_left.T, preferred_element_type=jnp.float32)
    )
    input_row_values = input_row_values.astype(jnp.bfloat16)
    scaled_rows = (scales * gradient_rows.astype(jnp.float32)).astype(jnp.bfloat16)
    scaled_low = (scales * backward_lowrank).astype(jnp.bfloat16)
    partial_results = [
        jnp.dot(incoming_rows.T, gate_reverse, preferred_element_type=jnp.float32),
        jnp.dot(lowrank_gate.T, gate_gradient, preferred_element_type=jnp.float32),
        jnp.dot(incoming_rows.T, upward_reverse, preferred_element_type=jnp.float32),
        jnp.dot(lowrank_upward.T, upward_gradient, preferred_element_type=jnp.float32),
        jnp.dot(hidden_activation.T, scaled_low, preferred_element_type=jnp.float32),
        jnp.dot(lowrank_hidden.T, scaled_rows, preferred_element_type=jnp.float32),
    ]
    adapter_products = adapter_scale * jnp.concatenate(
        [partial_result.reshape(-1) for partial_result in partial_results]
    )
    return (input_row_values, weight_row_values, adapter_products)


def shards(
    output_gradient,
    input_tokens,
    routes,
    combine,
    gate_matrix,
    upward_matrix,
    down_matrix,
    gate_adapter_left,
    gate_adapter_right,
    upward_adapter_left,
    upward_adapter_right,
    down_adapter_left,
    down_adapter_right,
):
    devices = lax.axis_size("exp")
    token_rows, model_width = output_gradient.shape
    top_k = routes.shape[1]
    capacity = max(2, min(token_rows, (2 * token_rows * top_k + devices - 1) // devices))
    slots_total = devices * capacity
    chosen = routes.reshape(-1)
    onehot = (chosen[:, None] == jnp.arange(devices, dtype=jnp.int32)[None, :]).astype(jnp.int32)
    earlier = jnp.cumsum(onehot, axis=0) - onehot
    target = chosen * capacity + jnp.sum(earlier * onehot, axis=1)
    owners = jnp.arange(chosen.shape[0], dtype=jnp.int32) // top_k
    send_inputs = (
        jnp.zeros((slots_total, model_width), jnp.bfloat16)
        .at[target]
        .set(input_tokens[owners])
        .reshape(devices, capacity, model_width)
    )
    send_grads = (
        jnp.zeros((slots_total, model_width), jnp.bfloat16)
        .at[target]
        .set(output_gradient[owners])
        .reshape(devices, capacity, model_width)
    )
    send_gates = (
        jnp.zeros((slots_total,), jnp.bfloat16)
        .at[target]
        .set(combine.reshape(-1))
        .reshape(devices, capacity)
    )
    gate_local = gate_matrix[0]
    upper_local = upward_matrix[0]
    down_local = down_matrix[0]
    got_inputs = lax.all_to_all(
        send_inputs, "exp", split_axis=0, concat_axis=0, tiled=True
    ).reshape(slots_total, model_width)
    saved_activations = expert_forward_pass(
        got_inputs,
        gate_local,
        upper_local,
        gate_adapter_left,
        gate_adapter_right,
        upward_adapter_left,
        upward_adapter_right,
        down_adapter_left,
    )
    got_grads, got_gates = (
        lax.all_to_all(send_grads, "exp", split_axis=0, concat_axis=0, tiled=True),
        lax.all_to_all(send_gates, "exp", split_axis=0, concat_axis=0, tiled=True),
    )
    got_grads = got_grads.reshape(slots_total, model_width)
    got_gates = got_gates.reshape(slots_total)
    input_row_values, weight_row_values, adapter_products = expert_reverse_pass(
        saved_activations,
        got_inputs,
        got_grads,
        got_gates,
        gate_local,
        upper_local,
        down_local,
        gate_adapter_left,
        gate_adapter_right,
        upward_adapter_left,
        upward_adapter_right,
        down_adapter_left,
        down_adapter_right,
    )
    back_inputs, back_weights = (
        lax.all_to_all(
            input_row_values.reshape(devices, capacity, model_width),
            "exp",
            split_axis=0,
            concat_axis=0,
            tiled=True,
        ),
        lax.all_to_all(
            weight_row_values.reshape(devices, capacity),
            "exp",
            split_axis=0,
            concat_axis=0,
            tiled=True,
        ),
    )
    returned = back_inputs.reshape(slots_total, model_width)[target].reshape(
        token_rows, top_k, model_width
    )
    grad_in = jnp.sum(returned.astype(jnp.float32), axis=1).astype(jnp.bfloat16)
    grad_combine = back_weights.reshape(slots_total)[target].reshape(token_rows, top_k)
    summed = lax.psum(adapter_products, "exp")
    share_length = adapter_products.shape[0] // devices
    grad_adapters = lax.dynamic_slice_in_dim(
        summed, lax.axis_index("exp") * share_length, share_length
    )
    return (grad_in, grad_combine, grad_adapters)


MESH = pl.DeviceIdType.MESH
CHUNKS = 4
LANES = 128


def nt(a, b):
    return lax.dot_general(a, b, (((1,), (1,)), ((), ())), preferred_element_type=jnp.float32)


def nn(a, b):
    return jnp.dot(a, b, preferred_element_type=jnp.float32)


def dense_kernel(
    n,
    line,
    grad_hbm,
    tok_hbm,
    routes_hbm,
    combine_hbm,
    gate_hbm,
    upper_hbm,
    down_hbm,
    gal_hbm,
    gar_hbm,
    ual_hbm,
    uar_hbm,
    dal_hbm,
    dar_hbm,
    out_in,
    out_comb,
    out_adapt,
    xbuf,
    gbuf,
    routes,
    comb,
    wcat,
    down,
    gal,
    ual,
    rcat,
    gar8,
    uar8,
    dal,
    dar8,
    pre_g,
    pre_u,
    raw,
    low8,
    xt,
    hidden,
    gcat,
    wrows,
    tbuf,
    aflat,
    ashare,
    pbuf,
    ra,
    rb,
    rc,
    ebuf,
    ea,
    eb,
    ec,
    load_sem,
    xs,
    xr,
    gs,
    gr,
    as_,
    ar,
    bs,
    br,
    cs,
    cr,
):
    t, width = tok_hbm.shape
    hid = gate_hbm.shape[2]
    rank = gar_hbm.shape[0]
    top = routes_hbm.shape[1]
    rep = LANES // rank
    rows = n * t
    half, quarter = n // 2, n // 4
    share = out_adapt.shape[0]
    step = width // CHUNKS

    me = lax.axis_index("exp")
    core, col, pos = lax.rem(me, 2), lax.rem(me // 2, 2), me // 4

    def index_of(c, x, z):
        return (lax.rem(pos + z, line) * 2 + lax.rem(col + x, 2)) * 2 + lax.rem(core + c, 2)

    def slot(c, x, z):
        return c * half + x * quarter + z

    sibling = index_of(1, 0, 0)
    across = index_of(0, 1, 0)
    along = [index_of(0, 0, dz) for dz in range(line)]

    loads = []

    def load(src, dst):
        copy = pltpu.make_async_copy(src, dst, load_sem.at[len(loads)])
        copy.start()
        loads.append(copy)
        return copy

    own_x = load(tok_hbm, xbuf.at[0])
    own_g = load(grad_hbm, gbuf.at[0, :, pl.ds(0, width)])
    own_r = load(routes_hbm, routes)
    own_c = load(combine_hbm, comb)
    load_al = [load(gal_hbm, gal), load(ual_hbm, ual)]
    load_gate = load(gate_hbm.at[0], wcat.at[:, pl.ds(0, hid)])
    load_rc = [
        load(gar_hbm, rcat.at[pl.ds(0, rank), pl.ds(0, hid)]),
        load(uar_hbm, rcat.at[pl.ds(rank, rank), pl.ds(hid, hid)]),
    ]
    load_upper = load(upper_hbm.at[0], wcat.at[:, pl.ds(hid, hid)])
    load_small = []
    for i in range(rep):
        load_small.append(load(gar_hbm, gar8.at[pl.ds(i * rank, rank)]))
        load_small.append(load(uar_hbm, uar8.at[pl.ds(i * rank, rank)]))
        load_small.append(load(dar_hbm, dar8.at[pl.ds(i * rank, rank)]))
    load_small.append(load(dal_hbm, dal))
    load_down = load(down_hbm.at[0], down)

    peers = [sibling, across] + along[1:]
    barrier = pltpu.get_barrier_semaphore()
    for peer in peers:
        pl.semaphore_signal(barrier, inc=1, device_id={"exp": peer}, device_id_type=MESH)
    pl.semaphore_wait(barrier, len(peers))

    def gather_copy(buf, send, recv, src, dst, peer):
        return pltpu.make_async_remote_copy(
            src_ref=buf.at[src],
            dst_ref=buf.at[dst],
            send_sem=send.at[dst],
            recv_sem=recv.at[dst],
            device_id={"exp": peer},
            device_id_type=MESH,
        )

    order = [dz for pair in zip(range(1, line), range(line - 1, 0, -1)) for dz in pair]
    order = list(dict.fromkeys(order))
    sent = []

    def send(bufs, src, dst, peer):
        copy = gather_copy(*bufs, src, dst, peer)
        copy.start()
        sent.append(copy)

    def arrived(bufs, s):
        gather_copy(*bufs, s, s, sibling).wait_recv()

    def own_phase(bufs):
        for dz in order:
            send(bufs, 0, slot(0, 0, line - dz), along[dz])
        send(bufs, 0, slot(0, 1, 0), across)
        send(bufs, 0, slot(1, 0, 0), sibling)

    def line_phase(bufs):
        for dz in order:
            arrived(bufs, slot(0, 0, dz))
            send(bufs, slot(0, 0, dz), slot(0, 1, dz), across)
            send(bufs, slot(0, 0, dz), slot(1, 0, dz), sibling)

    def across_phase(bufs):
        for dz in [0] + order:
            arrived(bufs, slot(0, 1, dz))
            send(bufs, slot(0, 1, dz), slot(1, 1, dz), sibling)

    def sibling_phase(bufs):
        for s in range(half, n):
            arrived(bufs, s)

    xb, gb = (xbuf, xs, xr), (gbuf, gs, gr)
    own_x.wait()
    own_phase(xb)
    own_g.wait()
    own_r.wait()
    own_c.wait()
    lanes_t = lax.broadcasted_iota(jnp.int32, (t, LANES), 1)
    chosen = routes[...]
    weights = comb[...].astype(jnp.float32)
    dense = jnp.zeros((t, LANES), jnp.float32)
    for k in range(top):
        dense = dense + jnp.where(lanes_t == chosen[:, k : k + 1], weights[:, k : k + 1], 0.0)
    gbuf[0, :, pl.ds(width, LANES)] = dense.astype(jnp.bfloat16)
    own_phase(gb)

    rcat[pl.ds(0, rank), pl.ds(hid, hid)] = jnp.zeros((rank, hid), jnp.bfloat16)
    rcat[pl.ds(rank, rank), pl.ds(0, hid)] = jnp.zeros((rank, hid), jnp.bfloat16)
    ashare[...] = jnp.zeros_like(ashare)
    line_phase(xb)
    for copy in load_al:
        copy.wait()
    wcat[:, pl.ds(2 * hid, LANES)] = jnp.concatenate(
        [gal[...], ual[...], jnp.zeros((width, LANES - 2 * rank), jnp.bfloat16)], axis=1
    )
    across_phase(xb)
    for copy in load_rc:
        copy.wait()
    load_gate.wait()
    load_upper.wait()
    sibling_phase(xb)

    line_phase(gb)
    x_all = xbuf[...].reshape(rows, width)
    low_cat = nn(x_all, wcat[:, pl.ds(2 * hid, LANES)])[:, : 2 * rank].astype(jnp.bfloat16)
    pre_g[...] = nn(x_all, wcat[:, pl.ds(0, hid)]) + adapter_scale * nn(low_cat, rcat[:, pl.ds(0, hid)])
    across_phase(gb)
    pre_u[...] = nn(x_all, wcat[:, pl.ds(hid, hid)]) + adapter_scale * nn(
        low_cat, rcat[:, pl.ds(hid, hid)]
    )
    xt[...] = x_all.T
    for copy in load_small:
        copy.wait()
    load_down.wait()
    sibling_phase(gb)

    g_all = gbuf[:, :, pl.ds(0, width)].reshape(rows, width)
    gates = gbuf[:, :, pl.ds(width, LANES)].reshape(rows, LANES).astype(jnp.float32)
    lanes_r = lax.broadcasted_iota(jnp.int32, (rows, LANES), 1)
    gate_col = jnp.sum(jnp.where(lanes_r == me, gates, 0.0), axis=1, keepdims=True)
    back_low8 = nt(g_all, dar8[...])
    back_rounded = back_low8[:, :rank].astype(jnp.bfloat16)
    raw[...] = nt(g_all, down[...]) + adapter_scale * nt(back_rounded, dal[...])
    low8[...] = (gate_col * back_low8).astype(jnp.bfloat16)
    wrows[...] = jnp.broadcast_to(gate_col, (rows, LANES))

    block = 16

    def pointwise(i, carry):
        here = pl.ds(pl.multiple_of(i * block, block), block)
        v, u, h = pre_g[here, :], pre_u[here, :], raw[here, :]
        s = jax.nn.sigmoid(v)
        hidden_here = (v * s * u).astype(jnp.bfloat16)
        hidden[here, :] = hidden_here
        hg = wrows[here, :][:, :1] * h
        gcat[here, pl.ds(0, hid)] = (hg * u * s * (1.0 + v * (1.0 - s))).astype(jnp.bfloat16)
        gcat[here, pl.ds(hid, hid)] = (hg * v * s).astype(jnp.bfloat16)
        w = jnp.sum(hidden_here.astype(jnp.float32) * h, axis=1, keepdims=True)
        lanes_b = lax.broadcasted_iota(jnp.int32, (block, LANES), 1)
        ebuf[i, pl.ds(ebuf.shape[1] - t, t), :] = jnp.where(lanes_b == me, w, 0.0).astype(jnp.bfloat16)
        return carry

    lax.fori_loop(0, rows // block, pointwise, 0)

    gb8 = nt(gcat[:, pl.ds(0, hid)], gar8[...])
    ub8 = nt(gcat[:, pl.ds(hid, hid)], uar8[...])
    backs = jnp.where(lanes_r < rank, gb8, jnp.where(lanes_r < 2 * rank, ub8, 0.0))
    backs = adapter_scale * backs.astype(jnp.bfloat16).astype(jnp.float32)
    gcat[:, pl.ds(2 * hid, LANES)] = backs.astype(jnp.bfloat16)

    def push(src, dst, send_sem, recv_sem, peer):
        copy = pltpu.make_async_remote_copy(
            src_ref=src,
            dst_ref=dst,
            send_sem=send_sem,
            recv_sem=recv_sem,
            device_id={"exp": peer},
            device_id_type=MESH,
        )
        return copy

    def views(i):
        if i < CHUNKS:
            return pbuf.at[i], ra.at[i], rb.at[i], rc.at[i]
        return ebuf, ea, eb, ec

    def start_a(i):
        p, a, b, c = views(i)
        copy = push(p.at[pl.ds(half, half)], a, as_.at[i], ar.at[i], sibling)
        copy.start()
        sent.append(copy)

    def add(p, q):
        return (p.astype(jnp.float32) + q.astype(jnp.float32)).astype(jnp.bfloat16)

    def stage_b(i):
        p, a, b, c = views(i)
        push(p.at[pl.ds(half, half)], a, as_.at[i], ar.at[i], sibling).wait_recv()
        p[pl.ds(quarter, quarter)] = add(p[pl.ds(quarter, quarter)], a[pl.ds(quarter, quarter)])
        copy = push(p.at[pl.ds(quarter, quarter)], b, bs.at[i], br.at[i], across)
        copy.start()
        sent.append(copy)
        p[pl.ds(0, quarter)] = add(p[pl.ds(0, quarter)], a[pl.ds(0, quarter)])

    def stage_c(i):
        p, a, b, c = views(i)
        push(p.at[pl.ds(quarter, quarter)], b, bs.at[i], br.at[i], across).wait_recv()
        p[pl.ds(0, quarter)] = add(p[pl.ds(0, quarter)], b[...])
        for dz in order:
            copy = push(p.at[dz], c.at[line - dz - 1], cs.at[i, dz - 1], cr.at[i, line - dz - 1], along[dz])
            copy.start()
            sent.append(copy)

    def total(i):
        p, a, b, c = views(i)
        value = p[0].astype(jnp.float32)
        for dz in range(1, line):
            push(p.at[dz], c.at[dz - 1], cs.at[i, dz - 1], cr.at[i, dz - 1], along[dz]).wait_recv()
            value = value + c[dz - 1].astype(jnp.float32)
        return value

    def compute_rows(i):
        piece = nt(gcat[...], wcat[pl.ds(i * step, step), :])
        pbuf[i] = piece.astype(jnp.bfloat16).reshape(n, t, step)

    def folded(value):
        count = value.shape[0] // rep
        sub = lax.broadcasted_iota(jnp.int32, (rep, LANES), 0)
        lane = lax.broadcasted_iota(jnp.int32, (rep, LANES), 1)
        mask = (lane // rank == sub).astype(jnp.float32) * adapter_scale
        return jnp.sum(value.reshape(count, rep, LANES) * mask[None], axis=1)

    def spread(start, value):
        pieces = value.shape[1] // LANES
        for k in range(pieces):
            aflat[pl.ds(start + k, rank, stride=pieces), :] = adapter_scale * value[:, k * LANES : (k + 1) * LANES]

    def compute_adapters():
        gate_rows_left, gate_rows_right = width * rank // LANES, hid * rank // LANES
        both = jnp.concatenate([gb8, ub8], axis=1).astype(jnp.bfloat16)
        tbuf[...] = nn(xt[...], both)
        at = 0
        aflat[pl.ds(at, gate_rows_left), :] = folded(tbuf[:, pl.ds(0, LANES)])
        at += gate_rows_left
        low_t = low_cat.T
        spread(at, nn(low_t[:rank], gcat[:, pl.ds(0, hid)]))
        at += gate_rows_right
        aflat[pl.ds(at, gate_rows_left), :] = folded(tbuf[:, pl.ds(LANES, LANES)])
        at += gate_rows_left
        spread(at, nn(low_t[rank:], gcat[:, pl.ds(hid, hid)]))
        at += gate_rows_right
        hid_all = hidden[...]
        aflat[pl.ds(at, gate_rows_right), :] = folded(nn(hid_all.T, low8[...]))
        at += gate_rows_right
        low_hidden = nn(hid_all, dal[...]).astype(jnp.bfloat16).astype(jnp.float32)
        low_hidden = (low_hidden * gate_col).astype(jnp.bfloat16)
        spread(at, nn(low_hidden.T, g_all))
        for d in range(n):
            ashare[d, pl.ds(0, share), :] = aflat[pl.ds(d * share, share), :]
        for c in range(2):
            for x in range(2):
                for z in range(line):
                    ebuf[slot(c, x, z), pl.ds(0, ashare.shape[1]), :] = ashare[index_of(c, x, z)].astype(
                        jnp.bfloat16
                    )

    plan = list(range(CHUNKS)) + [CHUNKS]
    for k in range(len(plan) + 2):
        if k < len(plan):
            if plan[k] < CHUNKS:
                compute_rows(plan[k])
            else:
                compute_adapters()
            start_a(plan[k])
        if 1 <= k <= len(plan):
            stage_b(plan[k - 1])
        if k >= 2:
            stage_c(plan[k - 2])

    for i in range(CHUNKS):
        out_in[:, pl.ds(i * step, step)] = total(i).astype(jnp.bfloat16)
    extra = total(CHUNKS)
    out_adapt[...] = extra[:share]
    w_rows = extra[ebuf.shape[1] - t :]
    lanes_k = lax.broadcasted_iota(jnp.int32, (t, top), 1)
    picked = jnp.zeros((t, top), jnp.float32)
    for k in range(top):
        value = jnp.sum(jnp.where(lanes_t == chosen[:, k : k + 1], w_rows, 0.0), axis=1, keepdims=True)
        picked = picked + jnp.where(lanes_k == k, value, 0.0)
    out_comb[...] = picked.astype(jnp.bfloat16)
    for copy in sent:
        copy.wait_send()


def dense_shards(*operands):
    grad, tok, routes, combine, gate, upper, down, gal, gar, ual, uar, dal, dar = operands
    n = lax.axis_size("exp")
    line = n // 4
    t, width = tok.shape
    top, hid, rank = routes.shape[1], gate.shape[2], gar.shape[0]
    rep = LANES // rank
    params = 3 * rank * (width + hid)
    share = params // n // LANES
    padded = -(-share // 16) * 16
    rows, half, quarter = n * t, n // 2, n // 4
    step = width // CHUNKS
    extra = padded + t
    bf, f32 = jnp.bfloat16, jnp.float32
    scratch = [
        pltpu.VMEM((n, t, width), bf),
        pltpu.VMEM((n, t, width + LANES), bf),
        pltpu.VMEM((t, top), jnp.int32),
        pltpu.VMEM((t, top), bf),
        pltpu.VMEM((width, 2 * hid + LANES), bf),
        pltpu.VMEM((hid, width), bf),
        pltpu.VMEM((width, rank), bf),
        pltpu.VMEM((width, rank), bf),
        pltpu.VMEM((2 * rank, 2 * hid), bf),
        pltpu.VMEM((LANES, hid), bf),
        pltpu.VMEM((LANES, hid), bf),
        pltpu.VMEM((hid, rank), bf),
        pltpu.VMEM((LANES, width), bf),
        pltpu.VMEM((rows, hid), f32),
        pltpu.VMEM((rows, hid), f32),
        pltpu.VMEM((rows, hid), f32),
        pltpu.VMEM((rows, LANES), bf),
        pltpu.VMEM((width, rows), bf),
        pltpu.VMEM((rows, hid), bf),
        pltpu.VMEM((rows, 2 * hid + LANES), bf),
        pltpu.VMEM((rows, LANES), f32),
        pltpu.VMEM((width, 2 * LANES), f32),
        pltpu.VMEM((share * n, LANES), f32),
        pltpu.VMEM((n, padded, LANES), f32),
        pltpu.VMEM((CHUNKS, n, t, step), bf),
        pltpu.VMEM((CHUNKS, half, t, step), bf),
        pltpu.VMEM((CHUNKS, quarter, t, step), bf),
        pltpu.VMEM((CHUNKS, line - 1, t, step), bf),
        pltpu.VMEM((n, extra, LANES), bf),
        pltpu.VMEM((half, extra, LANES), bf),
        pltpu.VMEM((quarter, extra, LANES), bf),
        pltpu.VMEM((line - 1, extra, LANES), bf),
        pltpu.SemaphoreType.DMA((12 + 3 * rep,)),
        pltpu.SemaphoreType.DMA((n,)),
        pltpu.SemaphoreType.DMA((n,)),
        pltpu.SemaphoreType.DMA((n,)),
        pltpu.SemaphoreType.DMA((n,)),
        pltpu.SemaphoreType.DMA((CHUNKS + 1,)),
        pltpu.SemaphoreType.DMA((CHUNKS + 1,)),
        pltpu.SemaphoreType.DMA((CHUNKS + 1,)),
        pltpu.SemaphoreType.DMA((CHUNKS + 1,)),
        pltpu.SemaphoreType.DMA((CHUNKS + 1, line - 1)),
        pltpu.SemaphoreType.DMA((CHUNKS + 1, line - 1)),
    ]
    grad_in, grad_combine, adapters = pl.pallas_call(
        functools.partial(dense_kernel, n, line),
        out_shape=(
            jax.ShapeDtypeStruct((t, width), bf),
            jax.ShapeDtypeStruct((t, top), bf),
            jax.ShapeDtypeStruct((share, LANES), f32),
        ),
        in_specs=[pl.BlockSpec(memory_space=pl.ANY)] * len(operands),
        out_specs=(pl.BlockSpec(memory_space=pltpu.VMEM),) * 3,
        scratch_shapes=scratch,
        compiler_params=pltpu.CompilerParams(
            collective_id=0, has_side_effects=True, vmem_limit_bytes=50 * 1024 * 1024
        ),
    )(*operands)
    return grad_in, grad_combine, adapters.reshape(-1)


def dense_fits(tokens, routes, gate, rank, groups, n):
    t, width = tokens.shape[0] // (groups * n), tokens.shape[1]
    top, hid = routes.shape[1], gate.shape[2]
    capacity = max(2, min(t, (2 * t * top + n - 1) // n))
    params = 3 * rank * (width + hid)
    return (
        capacity == t
        and t == 16
        and n % 4 == 0
        and 8 <= n <= LANES
        and gate.shape[0] == n
        and rank == 16
        and width % (CHUNKS * LANES) == 0
        and hid % LANES == 0
        and params % (n * LANES) == 0
    )


def solution(mesh):
    placed = (
        P(("grp", "exp"), None),
        P(("grp", "exp"), None),
        P(("grp", "exp"), None),
        P(("grp", "exp"), None),
        P("exp", None, None),
        P("exp", None, None),
        P("exp", None, None),
        P(),
        P(),
        P(),
        P(),
        P(),
        P(),
    )
    groups, n = mesh.shape["grp"], mesh.shape["exp"]

    def whole(*arrays):
        dense = dense_fits(arrays[1], arrays[2], arrays[4], arrays[8].shape[0], groups, n)
        return jax.shard_map(
            dense_shards if dense else shards,
            mesh=mesh,
            in_specs=placed,
            out_specs=(P(("grp", "exp"), None), P(("grp", "exp"), None), P(("grp", "exp"))),
            check_vma=False,
        )(*arrays)

    return whole
```

```python
import functools

import jax
import jax.numpy as jnp
from jax import lax
from jax.experimental import pallas as pl
from jax.experimental.pallas import tpu as pltpu
from jax.sharding import PartitionSpec as P

adapter_scale = 2.0


def expert_forward_pass(
    incoming_rows,
    gate_matrix,
    upward_matrix,
    gate_adapter_left,
    gate_adapter_right,
    upward_adapter_left,
    upward_adapter_right,
    down_adapter_left,
):
    lowrank_gate = jnp.dot(
        incoming_rows, gate_adapter_left, preferred_element_type=jnp.float32
    ).astype(jnp.bfloat16)
    lowrank_upward = jnp.dot(
        incoming_rows, upward_adapter_left, preferred_element_type=jnp.float32
    ).astype(jnp.bfloat16)
    gate_preactivation = jnp.dot(
        incoming_rows, gate_matrix, preferred_element_type=jnp.float32
    ) + adapter_scale * jnp.dot(
        lowrank_gate, gate_adapter_right, preferred_element_type=jnp.float32
    )
    upward_preactivation = jnp.dot(
        incoming_rows, upward_matrix, preferred_element_type=jnp.float32
    ) + adapter_scale * jnp.dot(
        lowrank_upward, upward_adapter_right, preferred_element_type=jnp.float32
    )
    hidden_activation = (jax.nn.silu(gate_preactivation) * upward_preactivation).astype(
        jnp.bfloat16
    )
    lowrank_hidden = jnp.dot(
        hidden_activation, down_adapter_left, preferred_element_type=jnp.float32
    ).astype(jnp.bfloat16)
    return (
        lowrank_gate,
        lowrank_upward,
        gate_preactivation,
        upward_preactivation,
        hidden_activation,
        lowrank_hidden,
    )


def expert_reverse_pass(
    saved_activations,
    incoming_rows,
    gradient_rows,
    gate_row_values,
    gate_matrix,
    upward_matrix,
    down_matrix,
    gate_adapter_left,
    gate_adapter_right,
    upward_adapter_left,
    upward_adapter_right,
    down_adapter_left,
    down_adapter_right,
):
    (
        lowrank_gate,
        lowrank_upward,
        gate_preactivation,
        upward_preactivation,
        hidden_activation,
        lowrank_hidden,
    ) = saved_activations
    backward_lowrank = jnp.dot(
        gradient_rows, down_adapter_right.T, preferred_element_type=jnp.float32
    )
    backward_truncated = backward_lowrank.astype(jnp.bfloat16)
    hidden_unscaled = jnp.dot(
        gradient_rows, down_matrix.T, preferred_element_type=jnp.float32
    ) + adapter_scale * jnp.dot(
        backward_truncated, down_adapter_left.T, preferred_element_type=jnp.float32
    )
    weight_row_values = jnp.sum(
        hidden_activation.astype(jnp.float32) * hidden_unscaled, axis=1
    ).astype(jnp.bfloat16)
    scales = gate_row_values.astype(jnp.float32)[:, None]
    hidden_grad = scales * hidden_unscaled
    logistic = jax.nn.sigmoid(gate_preactivation)
    gate_gradient = (
        hidden_grad
        * upward_preactivation
        * logistic
        * (1.0 + gate_preactivation * (1.0 - logistic))
    ).astype(jnp.bfloat16)
    upward_gradient = (hidden_grad * gate_preactivation * logistic).astype(jnp.bfloat16)
    gate_reverse = jnp.dot(
        gate_gradient, gate_adapter_right.T, preferred_element_type=jnp.float32
    ).astype(jnp.bfloat16)
    upward_reverse = jnp.dot(
        upward_gradient, upward_adapter_right.T, preferred_element_type=jnp.float32
    ).astype(jnp.bfloat16)
    input_row_values = jnp.dot(
        gate_gradient, gate_matrix.T, preferred_element_type=jnp.float32
    ) + jnp.dot(upward_gradient, upward_matrix.T, preferred_element_type=jnp.float32)
    input_row_values = input_row_values + adapter_scale * (
        jnp.dot(gate_reverse, gate_adapter_left.T, preferred_element_type=jnp.float32)
        + jnp.dot(upward_reverse, upward_adapter_left.T, preferred_element_type=jnp.float32)
    )
    input_row_values = input_row_values.astype(jnp.bfloat16)
    scaled_rows = (scales * gradient_rows.astype(jnp.float32)).astype(jnp.bfloat16)
    scaled_low = (scales * backward_lowrank).astype(jnp.bfloat16)
    partial_results = [
        jnp.dot(incoming_rows.T, gate_reverse, preferred_element_type=jnp.float32),
        jnp.dot(lowrank_gate.T, gate_gradient, preferred_element_type=jnp.float32),
        jnp.dot(incoming_rows.T, upward_reverse, preferred_element_type=jnp.float32),
        jnp.dot(lowrank_upward.T, upward_gradient, preferred_element_type=jnp.float32),
        jnp.dot(hidden_activation.T, scaled_low, preferred_element_type=jnp.float32),
        jnp.dot(lowrank_hidden.T, scaled_rows, preferred_element_type=jnp.float32),
    ]
    adapter_products = adapter_scale * jnp.concatenate(
        [partial_result.reshape(-1) for partial_result in partial_results]
    )
    return (input_row_values, weight_row_values, adapter_products)


def shards(
    output_gradient,
    input_tokens,
    routes,
    combine,
    gate_matrix,
    upward_matrix,
    down_matrix,
    gate_adapter_left,
    gate_adapter_right,
    upward_adapter_left,
    upward_adapter_right,
    down_adapter_left,
    down_adapter_right,
):
    devices = lax.axis_size("exp")
    token_rows, model_width = output_gradient.shape
    top_k = routes.shape[1]
    capacity = max(2, min(token_rows, (2 * token_rows * top_k + devices - 1) // devices))
    slots_total = devices * capacity
    chosen = routes.reshape(-1)
    onehot = (chosen[:, None] == jnp.arange(devices, dtype=jnp.int32)[None, :]).astype(jnp.int32)
    earlier = jnp.cumsum(onehot, axis=0) - onehot
    target = chosen * capacity + jnp.sum(earlier * onehot, axis=1)
    owners = jnp.arange(chosen.shape[0], dtype=jnp.int32) // top_k
    send_inputs = (
        jnp.zeros((slots_total, model_width), jnp.bfloat16)
        .at[target]
        .set(input_tokens[owners])
        .reshape(devices, capacity, model_width)
    )
    send_grads = (
        jnp.zeros((slots_total, model_width), jnp.bfloat16)
        .at[target]
        .set(output_gradient[owners])
        .reshape(devices, capacity, model_width)
    )
    send_gates = (
        jnp.zeros((slots_total,), jnp.bfloat16)
        .at[target]
        .set(combine.reshape(-1))
        .reshape(devices, capacity)
    )
    gate_local = gate_matrix[0]
    upper_local = upward_matrix[0]
    down_local = down_matrix[0]
    got_inputs = lax.all_to_all(
        send_inputs, "exp", split_axis=0, concat_axis=0, tiled=True
    ).reshape(slots_total, model_width)
    saved_activations = expert_forward_pass(
        got_inputs,
        gate_local,
        upper_local,
        gate_adapter_left,
        gate_adapter_right,
        upward_adapter_left,
        upward_adapter_right,
        down_adapter_left,
    )
    got_grads, got_gates = (
        lax.all_to_all(send_grads, "exp", split_axis=0, concat_axis=0, tiled=True),
        lax.all_to_all(send_gates, "exp", split_axis=0, concat_axis=0, tiled=True),
    )
    got_grads = got_grads.reshape(slots_total, model_width)
    got_gates = got_gates.reshape(slots_total)
    input_row_values, weight_row_values, adapter_products = expert_reverse_pass(
        saved_activations,
        got_inputs,
        got_grads,
        got_gates,
        gate_local,
        upper_local,
        down_local,
        gate_adapter_left,
        gate_adapter_right,
        upward_adapter_left,
        upward_adapter_right,
        down_adapter_left,
        down_adapter_right,
    )
    back_inputs, back_weights = (
        lax.all_to_all(
            input_row_values.reshape(devices, capacity, model_width),
            "exp",
            split_axis=0,
            concat_axis=0,
            tiled=True,
        ),
        lax.all_to_all(
            weight_row_values.reshape(devices, capacity),
            "exp",
            split_axis=0,
            concat_axis=0,
            tiled=True,
        ),
    )
    returned = back_inputs.reshape(slots_total, model_width)[target].reshape(
        token_rows, top_k, model_width
    )
    grad_in = jnp.sum(returned.astype(jnp.float32), axis=1).astype(jnp.bfloat16)
    grad_combine = back_weights.reshape(slots_total)[target].reshape(token_rows, top_k)
    summed = lax.psum(adapter_products, "exp")
    share_length = adapter_products.shape[0] // devices
    grad_adapters = lax.dynamic_slice_in_dim(
        summed, lax.axis_index("exp") * share_length, share_length
    )
    return (grad_in, grad_combine, grad_adapters)


MESH = pl.DeviceIdType.MESH
CHUNKS = 4
LANES = 128


def nt(a, b):
    return lax.dot_general(a, b, (((1,), (1,)), ((), ())), preferred_element_type=jnp.float32)


def nn(a, b):
    return jnp.dot(a, b, preferred_element_type=jnp.float32)


def dense_kernel(
    n,
    line,
    grad_hbm,
    tok_hbm,
    routes_hbm,
    comb,
    gate_hbm,
    upper_hbm,
    down_hbm,
    gal_hbm,
    gar_hbm,
    ual_hbm,
    uar_hbm,
    dal_hbm,
    dar_hbm,
    out_in,
    out_comb,
    out_adapt,
    xbuf,
    gbuf,
    routes,
    wcat,
    down,
    left,
    rcat,
    gar8,
    uar8,
    dal,
    dar8,
    pre_g,
    pre_u,
    raw,
    low8,
    xt,
    hidden,
    gcat,
    wrows,
    tbuf,
    aflat,
    ashare,
    pbuf,
    ra,
    rb,
    rc,
    ebuf,
    ea,
    eb,
    ec,
    load_sem,
    xs,
    xr,
    gs,
    gr,
    as_,
    ar,
    bs,
    br,
    cs,
    cr,
):
    t, width = tok_hbm.shape
    hid = gate_hbm.shape[2]
    rank = gar_hbm.shape[0]
    top = routes_hbm.shape[0]
    rep = LANES // rank
    rows = n * t
    half, quarter = n // 2, n // 4
    share = out_adapt.shape[0]
    step = width // CHUNKS

    me = lax.axis_index("exp")
    core, col, pos = lax.rem(me, 2), lax.rem(me // 2, 2), me // 4

    def index_of(c, x, z):
        return (lax.rem(pos + z, line) * 2 + lax.rem(col + x, 2)) * 2 + lax.rem(core + c, 2)

    def slot(c, x, z):
        return c * half + x * quarter + z

    sibling = index_of(1, 0, 0)
    across = index_of(0, 1, 0)
    along = [index_of(0, 0, dz) for dz in range(line)]

    loads = []

    def load(src, dst):
        copy = pltpu.make_async_copy(src, dst, load_sem.at[len(loads)])
        copy.start()
        loads.append(copy)
        return copy

    own_x = load(tok_hbm, xbuf.at[0])
    own_g = load(grad_hbm, gbuf.at[0, :, pl.ds(0, width)])
    own_r = load(routes_hbm, routes)
    load_al = [load(gal_hbm, left.at[pl.ds(0, rank)]), load(ual_hbm, left.at[pl.ds(rank, rank)])]
    load_gate = load(gate_hbm.at[0], wcat.at[:, pl.ds(0, hid)])
    load_rc = [
        load(gar_hbm, rcat.at[pl.ds(0, rank), pl.ds(0, hid)]),
        load(uar_hbm, rcat.at[pl.ds(rank, rank), pl.ds(hid, hid)]),
    ]
    load_upper = load(upper_hbm.at[0], wcat.at[:, pl.ds(hid, hid)])
    load_small = []
    for i in range(rep):
        load_small.append(load(gar_hbm, gar8.at[pl.ds(i * rank, rank)]))
        load_small.append(load(uar_hbm, uar8.at[pl.ds(i * rank, rank)]))
        load_small.append(load(dar_hbm, dar8.at[pl.ds(i * rank, rank)]))
    load_small.append(load(dal_hbm, dal))
    load_down = load(down_hbm.at[0], down)

    peers = [sibling, across] + along[1:]
    barrier = pltpu.get_barrier_semaphore()
    for peer in peers:
        pl.semaphore_signal(barrier, inc=1, device_id={"exp": peer}, device_id_type=MESH)
    pl.semaphore_wait(barrier, len(peers))

    def gather_copy(buf, send, recv, src, dst, peer):
        return pltpu.make_async_remote_copy(
            src_ref=buf.at[src],
            dst_ref=buf.at[dst],
            send_sem=send.at[dst],
            recv_sem=recv.at[dst],
            device_id={"exp": peer},
            device_id_type=MESH,
        )

    order = [dz for pair in zip(range(1, line), range(line - 1, 0, -1)) for dz in pair]
    order = list(dict.fromkeys(order))
    sent = []

    def send(bufs, src, dst, peer):
        copy = gather_copy(*bufs, src, dst, peer)
        copy.start()
        sent.append(copy)

    def arrived(bufs, s):
        gather_copy(*bufs, s, s, sibling).wait_recv()

    def own_phase(bufs):
        for dz in order:
            send(bufs, 0, slot(0, 0, line - dz), along[dz])
        send(bufs, 0, slot(0, 1, 0), across)
        send(bufs, 0, slot(1, 0, 0), sibling)

    def line_phase(bufs):
        for dz in order:
            arrived(bufs, slot(0, 0, dz))
            send(bufs, slot(0, 0, dz), slot(0, 1, dz), across)
            send(bufs, slot(0, 0, dz), slot(1, 0, dz), sibling)

    def across_phase(bufs):
        for dz in [0] + order:
            arrived(bufs, slot(0, 1, dz))
            send(bufs, slot(0, 1, dz), slot(1, 1, dz), sibling)

    def sibling_phase(bufs):
        for s in range(half, n):
            arrived(bufs, s)

    xb, gb = (xbuf, xs, xr), (gbuf, gs, gr)
    own_x.wait()
    own_phase(xb)
    own_g.wait()
    own_r.wait()
    lanes_t = lax.broadcasted_iota(jnp.int32, (t, LANES), 1)
    chosen = routes[...].T
    weights = comb[...].astype(jnp.float32).T
    dense = jnp.zeros((t, LANES), jnp.float32)
    for k in range(top):
        dense = dense + jnp.where(lanes_t == chosen[:, k : k + 1], weights[:, k : k + 1], 0.0)
    gbuf[0, :, pl.ds(width, LANES)] = dense.astype(jnp.bfloat16)
    own_phase(gb)

    rcat[pl.ds(0, rank), pl.ds(hid, hid)] = jnp.zeros((rank, hid), jnp.bfloat16)
    rcat[pl.ds(rank, rank), pl.ds(0, hid)] = jnp.zeros((rank, hid), jnp.bfloat16)
    ashare[...] = jnp.zeros_like(ashare)
    line_phase(xb)
    across_phase(xb)
    for copy in load_al + load_rc:
        copy.wait()
    load_gate.wait()
    load_upper.wait()
    sibling_phase(xb)

    line_phase(gb)
    x_all = xbuf[...].reshape(rows, width)
    low_cat = nt(x_all, left[...]).astype(jnp.bfloat16)
    pre_g[...] = nn(x_all, wcat[:, pl.ds(0, hid)]) + adapter_scale * nn(low_cat, rcat[:, pl.ds(0, hid)])
    across_phase(gb)
    pre_u[...] = nn(x_all, wcat[:, pl.ds(hid, hid)]) + adapter_scale * nn(
        low_cat, rcat[:, pl.ds(hid, hid)]
    )
    xt[...] = x_all.T
    for copy in load_small:
        copy.wait()
    load_down.wait()
    sibling_phase(gb)

    g_all = gbuf[:, :, pl.ds(0, width)].reshape(rows, width)
    gates = gbuf[:, :, pl.ds(width, LANES)].reshape(rows, LANES).astype(jnp.float32)
    lanes_r = lax.broadcasted_iota(jnp.int32, (rows, LANES), 1)
    gate_col = jnp.sum(jnp.where(lanes_r == me, gates, 0.0), axis=1, keepdims=True)
    back_low8 = nt(g_all, dar8[...])
    back_rounded = back_low8[:, :rank].astype(jnp.bfloat16)
    raw[...] = nt(g_all, down[...]) + adapter_scale * nn(back_rounded, dal[...])
    low8[...] = (gate_col * back_low8).astype(jnp.bfloat16)
    wrows[...] = jnp.broadcast_to(gate_col, (rows, LANES))

    block = 16

    def pointwise(i, carry):
        here = pl.ds(pl.multiple_of(i * block, block), block)
        v, u, h = pre_g[here, :], pre_u[here, :], raw[here, :]
        s = jax.nn.sigmoid(v)
        hidden_here = (v * s * u).astype(jnp.bfloat16)
        hidden[here, :] = hidden_here
        hg = wrows[here, :][:, :1] * h
        gcat[here, pl.ds(0, hid)] = (hg * u * s * (1.0 + v * (1.0 - s))).astype(jnp.bfloat16)
        gcat[here, pl.ds(hid, hid)] = (hg * v * s).astype(jnp.bfloat16)
        w = jnp.sum(hidden_here.astype(jnp.float32) * h, axis=1, keepdims=True)
        lanes_b = lax.broadcasted_iota(jnp.int32, (block, LANES), 1)
        ebuf[i, pl.ds(ebuf.shape[1] - t, t), :] = jnp.where(lanes_b == me, w, 0.0).astype(jnp.bfloat16)
        return carry

    lax.fori_loop(0, rows // block, pointwise, 0)

    gb8 = nt(gcat[:, pl.ds(0, hid)], gar8[...])
    ub8 = nt(gcat[:, pl.ds(hid, hid)], uar8[...])
    backs = jnp.where(lanes_r < rank, gb8, ub8)[:, : 2 * rank]
    backs = (adapter_scale * backs.astype(jnp.bfloat16).astype(jnp.float32)).astype(jnp.bfloat16)

    def push(src, dst, send_sem, recv_sem, peer):
        copy = pltpu.make_async_remote_copy(
            src_ref=src,
            dst_ref=dst,
            send_sem=send_sem,
            recv_sem=recv_sem,
            device_id={"exp": peer},
            device_id_type=MESH,
        )
        return copy

    def views(i):
        if i < CHUNKS:
            return pbuf.at[i], ra.at[i], rb.at[i], rc.at[i]
        return ebuf, ea, eb, ec

    def start_a(i):
        p, a, b, c = views(i)
        copy = push(p.at[pl.ds(half, half)], a, as_.at[i], ar.at[i], sibling)
        copy.start()
        sent.append(copy)

    def add(p, q):
        return (p.astype(jnp.float32) + q.astype(jnp.float32)).astype(jnp.bfloat16)

    def stage_b(i):
        p, a, b, c = views(i)
        push(p.at[pl.ds(half, half)], a, as_.at[i], ar.at[i], sibling).wait_recv()
        p[pl.ds(quarter, quarter)] = add(p[pl.ds(quarter, quarter)], a[pl.ds(quarter, quarter)])
        copy = push(p.at[pl.ds(quarter, quarter)], b, bs.at[i], br.at[i], across)
        copy.start()
        sent.append(copy)
        p[pl.ds(0, quarter)] = add(p[pl.ds(0, quarter)], a[pl.ds(0, quarter)])

    def stage_c(i):
        p, a, b, c = views(i)
        push(p.at[pl.ds(quarter, quarter)], b, bs.at[i], br.at[i], across).wait_recv()
        p[pl.ds(0, quarter)] = add(p[pl.ds(0, quarter)], b[...])
        for dz in order:
            copy = push(p.at[dz], c.at[line - dz - 1], cs.at[i, dz - 1], cr.at[i, line - dz - 1], along[dz])
            copy.start()
            sent.append(copy)

    def total(i):
        p, a, b, c = views(i)
        value = p[0].astype(jnp.float32)
        for dz in range(1, line):
            push(p.at[dz], c.at[dz - 1], cs.at[i, dz - 1], cr.at[i, dz - 1], along[dz]).wait_recv()
            value = value + c[dz - 1].astype(jnp.float32)
        return value

    def compute_rows(i):
        piece = nt(gcat[...], wcat[pl.ds(i * step, step), :])
        piece = piece + nn(backs, left[:, pl.ds(i * step, step)])
        pbuf[i] = piece.astype(jnp.bfloat16).reshape(n, t, step)

    def folded(value):
        count = value.shape[0] // rep
        sub = lax.broadcasted_iota(jnp.int32, (rep, LANES), 0)
        lane = lax.broadcasted_iota(jnp.int32, (rep, LANES), 1)
        mask = (lane // rank == sub).astype(jnp.float32) * adapter_scale
        return jnp.sum(value.reshape(count, rep, LANES) * mask[None], axis=1)

    def spread(start, value):
        pieces = value.shape[1] // LANES
        for k in range(pieces):
            aflat[pl.ds(start + k, rank, stride=pieces), :] = adapter_scale * value[:, k * LANES : (k + 1) * LANES]

    def compute_adapters():
        gate_rows_left, gate_rows_right = width * rank // LANES, hid * rank // LANES
        both = jnp.concatenate([gb8, ub8], axis=1).astype(jnp.bfloat16)
        tbuf[...] = nn(xt[...], both)
        at = 0
        aflat[pl.ds(at, gate_rows_left), :] = folded(tbuf[:, pl.ds(0, LANES)])
        at += gate_rows_left
        low_t = low_cat.T
        spread(at, nn(low_t[:rank], gcat[:, pl.ds(0, hid)]))
        at += gate_rows_right
        aflat[pl.ds(at, gate_rows_left), :] = folded(tbuf[:, pl.ds(LANES, LANES)])
        at += gate_rows_left
        spread(at, nn(low_t[rank:], gcat[:, pl.ds(hid, hid)]))
        at += gate_rows_right
        hid_all = hidden[...]
        aflat[pl.ds(at, gate_rows_right), :] = folded(nn(hid_all.T, low8[...]))
        at += gate_rows_right
        low_hidden = nt(hid_all, dal[...]).astype(jnp.bfloat16).astype(jnp.float32)
        low_hidden = (low_hidden * gate_col).astype(jnp.bfloat16)
        spread(at, nn(low_hidden.T, g_all))
        for d in range(n):
            ashare[d, pl.ds(0, share), :] = aflat[pl.ds(d * share, share), :]
        for c in range(2):
            for x in range(2):
                for z in range(line):
                    ebuf[slot(c, x, z), pl.ds(0, ashare.shape[1]), :] = ashare[index_of(c, x, z)].astype(
                        jnp.bfloat16
                    )

    plan = list(range(CHUNKS)) + [CHUNKS]
    for k in range(len(plan) + 2):
        if k < len(plan):
            if plan[k] < CHUNKS:
                compute_rows(plan[k])
            else:
                compute_adapters()
            start_a(plan[k])
        if 1 <= k <= len(plan):
            stage_b(plan[k - 1])
        if k >= 2:
            stage_c(plan[k - 2])

    for i in range(CHUNKS):
        out_in[:, pl.ds(i * step, step)] = total(i).astype(jnp.bfloat16)
    extra = total(CHUNKS)
    out_adapt[...] = extra[:share]
    w_rows = extra[ebuf.shape[1] - t :]
    lanes_k = lax.broadcasted_iota(jnp.int32, (t, top), 1)
    picked = jnp.zeros((t, top), jnp.float32)
    for k in range(top):
        value = jnp.sum(jnp.where(lanes_t == chosen[:, k : k + 1], w_rows, 0.0), axis=1, keepdims=True)
        picked = picked + jnp.where(lanes_k == k, value, 0.0)
    out_comb[...] = picked.T
    for copy in sent:
        copy.wait_send()


def dense_shards(*operands):
    grad, tok, routes, combine, gate, upper, down, gal, gar, ual, uar, dal, dar = operands
    n = lax.axis_size("exp")
    line = n // 4
    t, width = tok.shape
    top, hid, rank = routes.shape[1], gate.shape[2], gar.shape[0]
    rep = LANES // rank
    params = 3 * rank * (width + hid)
    share = params // n // LANES
    padded = -(-share // 16) * 16
    rows, half, quarter = n * t, n // 2, n // 4
    step = width // CHUNKS
    extra = padded + t
    bf, f32 = jnp.bfloat16, jnp.float32
    scratch = [
        pltpu.VMEM((n, t, width), bf),
        pltpu.VMEM((n, t, width + LANES), bf),
        pltpu.VMEM((top, t), jnp.int32),
        pltpu.VMEM((width, 2 * hid), bf),
        pltpu.VMEM((hid, width), bf),
        pltpu.VMEM((2 * rank, width), bf),
        pltpu.VMEM((2 * rank, 2 * hid), bf),
        pltpu.VMEM((LANES, hid), bf),
        pltpu.VMEM((LANES, hid), bf),
        pltpu.VMEM((rank, hid), bf),
        pltpu.VMEM((LANES, width), bf),
        pltpu.VMEM((rows, hid), f32),
        pltpu.VMEM((rows, hid), f32),
        pltpu.VMEM((rows, hid), f32),
        pltpu.VMEM((rows, LANES), bf),
        pltpu.VMEM((width, rows), bf),
        pltpu.VMEM((rows, hid), bf),
        pltpu.VMEM((rows, 2 * hid), bf),
        pltpu.VMEM((rows, LANES), f32),
        pltpu.VMEM((width, 2 * LANES), f32),
        pltpu.VMEM((share * n, LANES), f32),
        pltpu.VMEM((n, padded, LANES), f32),
        pltpu.VMEM((CHUNKS, n, t, step), bf),
        pltpu.VMEM((CHUNKS, half, t, step), bf),
        pltpu.VMEM((CHUNKS, quarter, t, step), bf),
        pltpu.VMEM((CHUNKS, line - 1, t, step), bf),
        pltpu.VMEM((n, extra, LANES), bf),
        pltpu.VMEM((half, extra, LANES), bf),
        pltpu.VMEM((quarter, extra, LANES), bf),
        pltpu.VMEM((line - 1, extra, LANES), bf),
        pltpu.SemaphoreType.DMA((11 + 3 * rep,)),
        pltpu.SemaphoreType.DMA((n,)),
        pltpu.SemaphoreType.DMA((n,)),
        pltpu.SemaphoreType.DMA((n,)),
        pltpu.SemaphoreType.DMA((n,)),
        pltpu.SemaphoreType.DMA((CHUNKS + 1,)),
        pltpu.SemaphoreType.DMA((CHUNKS + 1,)),
        pltpu.SemaphoreType.DMA((CHUNKS + 1,)),
        pltpu.SemaphoreType.DMA((CHUNKS + 1,)),
        pltpu.SemaphoreType.DMA((CHUNKS + 1, line - 1)),
        pltpu.SemaphoreType.DMA((CHUNKS + 1, line - 1)),
    ]
    grad_in, grad_combine, adapters = pl.pallas_call(
        functools.partial(dense_kernel, n, line),
        out_shape=(
            jax.ShapeDtypeStruct((t, width), bf),
            jax.ShapeDtypeStruct((top, t), f32),
            jax.ShapeDtypeStruct((share, LANES), f32),
        ),
        in_specs=[pl.BlockSpec(memory_space=pltpu.VMEM if i == 3 else pl.ANY) for i in range(13)],
        out_specs=(pl.BlockSpec(memory_space=pltpu.VMEM),) * 3,
        scratch_shapes=scratch,
        compiler_params=pltpu.CompilerParams(
            collective_id=0, has_side_effects=True, vmem_limit_bytes=62 * 1024 * 1024
        ),
    )(grad, tok, routes.T, combine.T, gate, upper, down, gal.T, gar, ual.T, uar, dal.T, dar)
    return grad_in, grad_combine.astype(bf).T, adapters.reshape(-1)


def dense_fits(tokens, routes, gate, rank, groups, n):
    t, width = tokens.shape[0] // (groups * n), tokens.shape[1]
    top, hid = routes.shape[1], gate.shape[2]
    capacity = max(2, min(t, (2 * t * top + n - 1) // n))
    params = 3 * rank * (width + hid)
    return (
        capacity == t
        and t == 16
        and n % 4 == 0
        and 8 <= n <= LANES
        and gate.shape[0] == n
        and rank == 16
        and width % (CHUNKS * LANES) == 0
        and hid % LANES == 0
        and params % (n * LANES) == 0
    )


def solution(mesh):
    placed = (
        P(("grp", "exp"), None),
        P(("grp", "exp"), None),
        P(("grp", "exp"), None),
        P(("grp", "exp"), None),
        P("exp", None, None),
        P("exp", None, None),
        P("exp", None, None),
        P(),
        P(),
        P(),
        P(),
        P(),
        P(),
    )
    groups, n = mesh.shape["grp"], mesh.shape["exp"]

    def whole(*arrays):
        dense = dense_fits(arrays[1], arrays[2], arrays[4], arrays[8].shape[0], groups, n)
        return jax.shard_map(
            dense_shards if dense else shards,
            mesh=mesh,
            in_specs=placed,
            out_specs=(P(("grp", "exp"), None), P(("grp", "exp"), None), P(("grp", "exp"))),
            check_vma=False,
        )(*arrays)

    return whole
```

```python
import functools

import jax
import jax.numpy as jnp
from jax import lax
from jax.experimental import pallas as pl
from jax.experimental.pallas import tpu as pltpu
from jax.sharding import PartitionSpec as P

adapter_scale = 2.0


def expert_forward_pass(
    incoming_rows,
    gate_matrix,
    upward_matrix,
    gate_adapter_left,
    gate_adapter_right,
    upward_adapter_left,
    upward_adapter_right,
    down_adapter_left,
):
    lowrank_gate = jnp.dot(
        incoming_rows, gate_adapter_left, preferred_element_type=jnp.float32
    ).astype(jnp.bfloat16)
    lowrank_upward = jnp.dot(
        incoming_rows, upward_adapter_left, preferred_element_type=jnp.float32
    ).astype(jnp.bfloat16)
    gate_preactivation = jnp.dot(
        incoming_rows, gate_matrix, preferred_element_type=jnp.float32
    ) + adapter_scale * jnp.dot(
        lowrank_gate, gate_adapter_right, preferred_element_type=jnp.float32
    )
    upward_preactivation = jnp.dot(
        incoming_rows, upward_matrix, preferred_element_type=jnp.float32
    ) + adapter_scale * jnp.dot(
        lowrank_upward, upward_adapter_right, preferred_element_type=jnp.float32
    )
    hidden_activation = (jax.nn.silu(gate_preactivation) * upward_preactivation).astype(
        jnp.bfloat16
    )
    lowrank_hidden = jnp.dot(
        hidden_activation, down_adapter_left, preferred_element_type=jnp.float32
    ).astype(jnp.bfloat16)
    return (
        lowrank_gate,
        lowrank_upward,
        gate_preactivation,
        upward_preactivation,
        hidden_activation,
        lowrank_hidden,
    )


def expert_reverse_pass(
    saved_activations,
    incoming_rows,
    gradient_rows,
    gate_row_values,
    gate_matrix,
    upward_matrix,
    down_matrix,
    gate_adapter_left,
    gate_adapter_right,
    upward_adapter_left,
    upward_adapter_right,
    down_adapter_left,
    down_adapter_right,
):
    (
        lowrank_gate,
        lowrank_upward,
        gate_preactivation,
        upward_preactivation,
        hidden_activation,
        lowrank_hidden,
    ) = saved_activations
    backward_lowrank = jnp.dot(
        gradient_rows, down_adapter_right.T, preferred_element_type=jnp.float32
    )
    backward_truncated = backward_lowrank.astype(jnp.bfloat16)
    hidden_unscaled = jnp.dot(
        gradient_rows, down_matrix.T, preferred_element_type=jnp.float32
    ) + adapter_scale * jnp.dot(
        backward_truncated, down_adapter_left.T, preferred_element_type=jnp.float32
    )
    weight_row_values = jnp.sum(
        hidden_activation.astype(jnp.float32) * hidden_unscaled, axis=1
    ).astype(jnp.bfloat16)
    scales = gate_row_values.astype(jnp.float32)[:, None]
    hidden_grad = scales * hidden_unscaled
    logistic = jax.nn.sigmoid(gate_preactivation)
    gate_gradient = (
        hidden_grad
        * upward_preactivation
        * logistic
        * (1.0 + gate_preactivation * (1.0 - logistic))
    ).astype(jnp.bfloat16)
    upward_gradient = (hidden_grad * gate_preactivation * logistic).astype(jnp.bfloat16)
    gate_reverse = jnp.dot(
        gate_gradient, gate_adapter_right.T, preferred_element_type=jnp.float32
    ).astype(jnp.bfloat16)
    upward_reverse = jnp.dot(
        upward_gradient, upward_adapter_right.T, preferred_element_type=jnp.float32
    ).astype(jnp.bfloat16)
    input_row_values = jnp.dot(
        gate_gradient, gate_matrix.T, preferred_element_type=jnp.float32
    ) + jnp.dot(upward_gradient, upward_matrix.T, preferred_element_type=jnp.float32)
    input_row_values = input_row_values + adapter_scale * (
        jnp.dot(gate_reverse, gate_adapter_left.T, preferred_element_type=jnp.float32)
        + jnp.dot(upward_reverse, upward_adapter_left.T, preferred_element_type=jnp.float32)
    )
    input_row_values = input_row_values.astype(jnp.bfloat16)
    scaled_rows = (scales * gradient_rows.astype(jnp.float32)).astype(jnp.bfloat16)
    scaled_low = (scales * backward_lowrank).astype(jnp.bfloat16)
    partial_results = [
        jnp.dot(incoming_rows.T, gate_reverse, preferred_element_type=jnp.float32),
        jnp.dot(lowrank_gate.T, gate_gradient, preferred_element_type=jnp.float32),
        jnp.dot(incoming_rows.T, upward_reverse, preferred_element_type=jnp.float32),
        jnp.dot(lowrank_upward.T, upward_gradient, preferred_element_type=jnp.float32),
        jnp.dot(hidden_activation.T, scaled_low, preferred_element_type=jnp.float32),
        jnp.dot(lowrank_hidden.T, scaled_rows, preferred_element_type=jnp.float32),
    ]
    adapter_products = adapter_scale * jnp.concatenate(
        [partial_result.reshape(-1) for partial_result in partial_results]
    )
    return (input_row_values, weight_row_values, adapter_products)


def shards(
    output_gradient,
    input_tokens,
    routes,
    combine,
    gate_matrix,
    upward_matrix,
    down_matrix,
    gate_adapter_left,
    gate_adapter_right,
    upward_adapter_left,
    upward_adapter_right,
    down_adapter_left,
    down_adapter_right,
):
    devices = lax.axis_size("exp")
    token_rows, model_width = output_gradient.shape
    top_k = routes.shape[1]
    capacity = max(2, min(token_rows, (2 * token_rows * top_k + devices - 1) // devices))
    slots_total = devices * capacity
    chosen = routes.reshape(-1)
    onehot = (chosen[:, None] == jnp.arange(devices, dtype=jnp.int32)[None, :]).astype(jnp.int32)
    earlier = jnp.cumsum(onehot, axis=0) - onehot
    target = chosen * capacity + jnp.sum(earlier * onehot, axis=1)
    owners = jnp.arange(chosen.shape[0], dtype=jnp.int32) // top_k
    send_inputs = (
        jnp.zeros((slots_total, model_width), jnp.bfloat16)
        .at[target]
        .set(input_tokens[owners])
        .reshape(devices, capacity, model_width)
    )
    send_grads = (
        jnp.zeros((slots_total, model_width), jnp.bfloat16)
        .at[target]
        .set(output_gradient[owners])
        .reshape(devices, capacity, model_width)
    )
    send_gates = (
        jnp.zeros((slots_total,), jnp.bfloat16)
        .at[target]
        .set(combine.reshape(-1))
        .reshape(devices, capacity)
    )
    gate_local = gate_matrix[0]
    upper_local = upward_matrix[0]
    down_local = down_matrix[0]
    got_inputs = lax.all_to_all(
        send_inputs, "exp", split_axis=0, concat_axis=0, tiled=True
    ).reshape(slots_total, model_width)
    saved_activations = expert_forward_pass(
        got_inputs,
        gate_local,
        upper_local,
        gate_adapter_left,
        gate_adapter_right,
        upward_adapter_left,
        upward_adapter_right,
        down_adapter_left,
    )
    got_grads, got_gates = (
        lax.all_to_all(send_grads, "exp", split_axis=0, concat_axis=0, tiled=True),
        lax.all_to_all(send_gates, "exp", split_axis=0, concat_axis=0, tiled=True),
    )
    got_grads = got_grads.reshape(slots_total, model_width)
    got_gates = got_gates.reshape(slots_total)
    input_row_values, weight_row_values, adapter_products = expert_reverse_pass(
        saved_activations,
        got_inputs,
        got_grads,
        got_gates,
        gate_local,
        upper_local,
        down_local,
        gate_adapter_left,
        gate_adapter_right,
        upward_adapter_left,
        upward_adapter_right,
        down_adapter_left,
        down_adapter_right,
    )
    back_inputs, back_weights = (
        lax.all_to_all(
            input_row_values.reshape(devices, capacity, model_width),
            "exp",
            split_axis=0,
            concat_axis=0,
            tiled=True,
        ),
        lax.all_to_all(
            weight_row_values.reshape(devices, capacity),
            "exp",
            split_axis=0,
            concat_axis=0,
            tiled=True,
        ),
    )
    returned = back_inputs.reshape(slots_total, model_width)[target].reshape(
        token_rows, top_k, model_width
    )
    grad_in = jnp.sum(returned.astype(jnp.float32), axis=1).astype(jnp.bfloat16)
    grad_combine = back_weights.reshape(slots_total)[target].reshape(token_rows, top_k)
    summed = lax.psum(adapter_products, "exp")
    share_length = adapter_products.shape[0] // devices
    grad_adapters = lax.dynamic_slice_in_dim(
        summed, lax.axis_index("exp") * share_length, share_length
    )
    return (grad_in, grad_combine, grad_adapters)


MESH = pl.DeviceIdType.MESH
CHUNKS = 2
PARTS = 2
LANES = 128


def nt(a, b):
    return lax.dot_general(a, b, (((1,), (1,)), ((), ())), preferred_element_type=jnp.float32)


def nn(a, b):
    return jnp.dot(a, b, preferred_element_type=jnp.float32)


def dense_kernel(
    n,
    line,
    grad_hbm,
    tok_hbm,
    routes_hbm,
    comb,
    gate_hbm,
    upper_hbm,
    down_hbm,
    gal_hbm,
    gar_hbm,
    ual_hbm,
    uar_hbm,
    dal_hbm,
    dar_hbm,
    out_in,
    out_comb,
    out_adapt,
    xbuf,
    gbuf,
    routes,
    wcat,
    down,
    left,
    rcat,
    gar8,
    uar8,
    dal,
    dar8,
    pre_g,
    pre_u,
    raw,
    low8,
    xt,
    hidden,
    gcat,
    wrows,
    tbuf,
    aflat,
    ashare,
    pbuf,
    ra,
    rb,
    rc,
    ebuf,
    ea,
    eb,
    ec,
    load_sem,
    xs,
    xr,
    gs,
    gr,
    as_,
    ar,
    bs,
    br,
    cs,
    cr,
):
    t, width = tok_hbm.shape
    hid = gate_hbm.shape[2]
    rank = gar_hbm.shape[0]
    top = routes_hbm.shape[0]
    rep = LANES // rank
    rows = n * t
    half, quarter = n // 2, n // 4
    share = out_adapt.shape[0]
    step = width // CHUNKS

    me = lax.axis_index("exp")
    core, col, pos = lax.rem(me, 2), lax.rem(me // 2, 2), me // 4

    def index_of(c, x, z):
        return (lax.rem(pos + z, line) * 2 + lax.rem(col + x, 2)) * 2 + lax.rem(core + c, 2)

    def slot(c, x, z):
        return c * half + x * quarter + z

    sibling = index_of(1, 0, 0)
    across = index_of(0, 1, 0)
    along = [index_of(0, 0, dz) for dz in range(line)]

    loads = []

    def load(src, dst):
        copy = pltpu.make_async_copy(src, dst, load_sem.at[len(loads)])
        copy.start()
        loads.append(copy)
        return copy

    own_x = load(tok_hbm, xbuf.at[0])
    own_g = load(grad_hbm, gbuf.at[0, :, pl.ds(0, width)])
    own_r = load(routes_hbm, routes)
    load_al = [load(gal_hbm, left.at[pl.ds(0, rank)]), load(ual_hbm, left.at[pl.ds(rank, rank)])]
    load_gate = load(gate_hbm.at[0], wcat.at[:, pl.ds(0, hid)])
    load_rc = [
        load(gar_hbm, rcat.at[pl.ds(0, rank), pl.ds(0, hid)]),
        load(uar_hbm, rcat.at[pl.ds(rank, rank), pl.ds(hid, hid)]),
    ]
    load_upper = load(upper_hbm.at[0], wcat.at[:, pl.ds(hid, hid)])
    load_small = []
    for i in range(rep):
        load_small.append(load(gar_hbm, gar8.at[pl.ds(i * rank, rank)]))
        load_small.append(load(uar_hbm, uar8.at[pl.ds(i * rank, rank)]))
        load_small.append(load(dar_hbm, dar8.at[pl.ds(i * rank, rank)]))
    load_small.append(load(dal_hbm, dal))
    load_down = load(down_hbm.at[0], down)

    peers = [sibling, across] + along[1:]
    barrier = pltpu.get_barrier_semaphore()
    for peer in peers:
        pl.semaphore_signal(barrier, inc=1, device_id={"exp": peer}, device_id_type=MESH)
    pl.semaphore_wait(barrier, len(peers))

    def gather_copy(buf, first, size, part, send, recv, src, dst, peer):
        return pltpu.make_async_remote_copy(
            src_ref=buf.at[src, :, pl.ds(first, size)],
            dst_ref=buf.at[dst, :, pl.ds(first, size)],
            send_sem=send.at[part, dst],
            recv_sem=recv.at[part, dst],
            device_id={"exp": peer},
            device_id_type=MESH,
        )

    order = [dz for pair in zip(range(1, line), range(line - 1, 0, -1)) for dz in pair]
    order = list(dict.fromkeys(order))
    sent = []

    def send(bufs, src, dst, peer):
        copy = gather_copy(*bufs, src, dst, peer)
        copy.start()
        sent.append(copy)

    def arrived(bufs, s):
        gather_copy(*bufs, s, s, sibling).wait_recv()

    def own_phase(bufs):
        for dz in order:
            send(bufs, 0, slot(0, 0, line - dz), along[dz])
        send(bufs, 0, slot(0, 1, 0), across)
        send(bufs, 0, slot(1, 0, 0), sibling)

    def line_phase(bufs):
        for dz in order:
            arrived(bufs, slot(0, 0, dz))
            send(bufs, slot(0, 0, dz), slot(0, 1, dz), across)
            send(bufs, slot(0, 0, dz), slot(1, 0, dz), sibling)

    def across_phase(bufs):
        for dz in [0] + order:
            arrived(bufs, slot(0, 1, dz))
            send(bufs, slot(0, 1, dz), slot(1, 1, dz), sibling)

    def sibling_phase(bufs):
        for s in range(half, n):
            arrived(bufs, s)

    size = width // PARTS
    x_parts = [(xbuf, i * size, size, i, xs, xr) for i in range(PARTS)]
    g_parts = [
        (gbuf, i * size, size + (LANES if i == PARTS - 1 else 0), i, gs, gr) for i in range(PARTS)
    ]
    own_x.wait()
    for part in x_parts:
        own_phase(part)
    own_g.wait()
    own_r.wait()
    lanes_t = lax.broadcasted_iota(jnp.int32, (t, LANES), 1)
    chosen = routes[...].T
    weights = comb[...].astype(jnp.float32).T
    dense = jnp.zeros((t, LANES), jnp.float32)
    for k in range(top):
        dense = dense + jnp.where(lanes_t == chosen[:, k : k + 1], weights[:, k : k + 1], 0.0)
    gbuf[0, :, pl.ds(width, LANES)] = dense.astype(jnp.bfloat16)

    rcat[pl.ds(0, rank), pl.ds(hid, hid)] = jnp.zeros((rank, hid), jnp.bfloat16)
    rcat[pl.ds(rank, rank), pl.ds(0, hid)] = jnp.zeros((rank, hid), jnp.bfloat16)
    ashare[...] = jnp.zeros_like(ashare)
    for i in range(PARTS):
        line_phase(x_parts[i])
        own_phase(g_parts[i])
        if i > 0:
            across_phase(x_parts[i - 1])
    line_phase(g_parts[0])
    across_phase(x_parts[PARTS - 1])
    for copy in load_al + load_rc:
        copy.wait()
    load_gate.wait()
    load_upper.wait()
    for part in x_parts:
        sibling_phase(part)

    x_all = xbuf[...].reshape(rows, width)
    low_cat = nt(x_all, left[...]).astype(jnp.bfloat16)
    pre_g[...] = nn(x_all, wcat[:, pl.ds(0, hid)]) + adapter_scale * nn(low_cat, rcat[:, pl.ds(0, hid)])
    for i in range(1, PARTS):
        line_phase(g_parts[i])
        across_phase(g_parts[i - 1])
    pre_u[...] = nn(x_all, wcat[:, pl.ds(hid, hid)]) + adapter_scale * nn(
        low_cat, rcat[:, pl.ds(hid, hid)]
    )
    across_phase(g_parts[PARTS - 1])
    xt[...] = x_all.T
    for copy in load_small:
        copy.wait()
    load_down.wait()
    for part in g_parts:
        sibling_phase(part)

    g_all = gbuf[:, :, pl.ds(0, width)].reshape(rows, width)
    gates = gbuf[:, :, pl.ds(width, LANES)].reshape(rows, LANES).astype(jnp.float32)
    lanes_r = lax.broadcasted_iota(jnp.int32, (rows, LANES), 1)
    gate_col = jnp.sum(jnp.where(lanes_r == me, gates, 0.0), axis=1, keepdims=True)
    back_low8 = nt(g_all, dar8[...])
    back_rounded = back_low8[:, :rank].astype(jnp.bfloat16)
    raw[...] = nt(g_all, down[...]) + adapter_scale * nn(back_rounded, dal[...])
    low8[...] = (gate_col * back_low8).astype(jnp.bfloat16)
    wrows[...] = jnp.broadcast_to(gate_col, (rows, LANES))

    block = 16

    def pointwise(i, carry):
        here = pl.ds(pl.multiple_of(i * block, block), block)
        v, u, h = pre_g[here, :], pre_u[here, :], raw[here, :]
        s = jax.nn.sigmoid(v)
        hidden_here = (v * s * u).astype(jnp.bfloat16)
        hidden[here, :] = hidden_here
        hg = wrows[here, :][:, :1] * h
        gcat[here, pl.ds(0, hid)] = (hg * u * s * (1.0 + v * (1.0 - s))).astype(jnp.bfloat16)
        gcat[here, pl.ds(hid, hid)] = (hg * v * s).astype(jnp.bfloat16)
        w = jnp.sum(hidden_here.astype(jnp.float32) * h, axis=1, keepdims=True)
        lanes_b = lax.broadcasted_iota(jnp.int32, (block, LANES), 1)
        ebuf[i, pl.ds(ebuf.shape[1] - t, t), :] = jnp.where(lanes_b == me, w, 0.0).astype(jnp.bfloat16)
        return carry

    lax.fori_loop(0, rows // block, pointwise, 0)

    gb8 = nt(gcat[:, pl.ds(0, hid)], gar8[...])
    ub8 = nt(gcat[:, pl.ds(hid, hid)], uar8[...])
    backs = jnp.where(lanes_r < rank, gb8, ub8)[:, : 2 * rank]
    backs = (adapter_scale * backs.astype(jnp.bfloat16).astype(jnp.float32)).astype(jnp.bfloat16)

    def push(src, dst, send_sem, recv_sem, peer):
        copy = pltpu.make_async_remote_copy(
            src_ref=src,
            dst_ref=dst,
            send_sem=send_sem,
            recv_sem=recv_sem,
            device_id={"exp": peer},
            device_id_type=MESH,
        )
        return copy

    def views(i):
        if i < CHUNKS:
            return pbuf.at[i], ra.at[i], rb.at[i], rc.at[i]
        return ebuf, ea, eb, ec

    def start_a(i):
        p, a, b, c = views(i)
        copy = push(p.at[pl.ds(half, half)], a, as_.at[i], ar.at[i], sibling)
        copy.start()
        sent.append(copy)

    def add(p, q):
        return (p.astype(jnp.float32) + q.astype(jnp.float32)).astype(jnp.bfloat16)

    def stage_b(i):
        p, a, b, c = views(i)
        push(p.at[pl.ds(half, half)], a, as_.at[i], ar.at[i], sibling).wait_recv()
        p[pl.ds(quarter, quarter)] = add(p[pl.ds(quarter, quarter)], a[pl.ds(quarter, quarter)])
        copy = push(p.at[pl.ds(quarter, quarter)], b, bs.at[i], br.at[i], across)
        copy.start()
        sent.append(copy)
        p[pl.ds(0, quarter)] = add(p[pl.ds(0, quarter)], a[pl.ds(0, quarter)])

    def stage_c(i):
        p, a, b, c = views(i)
        push(p.at[pl.ds(quarter, quarter)], b, bs.at[i], br.at[i], across).wait_recv()
        p[pl.ds(0, quarter)] = add(p[pl.ds(0, quarter)], b[...])
        for dz in order:
            copy = push(p.at[dz], c.at[line - dz - 1], cs.at[i, dz - 1], cr.at[i, line - dz - 1], along[dz])
            copy.start()
            sent.append(copy)

    def total(i):
        p, a, b, c = views(i)
        value = p[0].astype(jnp.float32)
        for dz in range(1, line):
            push(p.at[dz], c.at[dz - 1], cs.at[i, dz - 1], cr.at[i, dz - 1], along[dz]).wait_recv()
            value = value + c[dz - 1].astype(jnp.float32)
        return value

    def compute_rows(i):
        piece = nt(gcat[...], wcat[pl.ds(i * step, step), :])
        piece = piece + nn(backs, left[:, pl.ds(i * step, step)])
        pbuf[i] = piece.astype(jnp.bfloat16).reshape(n, t, step)

    def folded(value):
        count = value.shape[0] // rep
        sub = lax.broadcasted_iota(jnp.int32, (rep, LANES), 0)
        lane = lax.broadcasted_iota(jnp.int32, (rep, LANES), 1)
        mask = (lane // rank == sub).astype(jnp.float32) * adapter_scale
        return jnp.sum(value.reshape(count, rep, LANES) * mask[None], axis=1)

    def spread(start, value):
        pieces = value.shape[1] // LANES
        for k in range(pieces):
            aflat[pl.ds(start + k, rank, stride=pieces), :] = adapter_scale * value[:, k * LANES : (k + 1) * LANES]

    def compute_adapters():
        gate_rows_left, gate_rows_right = width * rank // LANES, hid * rank // LANES
        both = jnp.concatenate([gb8, ub8], axis=1).astype(jnp.bfloat16)
        tbuf[...] = nn(xt[...], both)
        at = 0
        aflat[pl.ds(at, gate_rows_left), :] = folded(tbuf[:, pl.ds(0, LANES)])
        at += gate_rows_left
        low_t = low_cat.T
        spread(at, nn(low_t[:rank], gcat[:, pl.ds(0, hid)]))
        at += gate_rows_right
        aflat[pl.ds(at, gate_rows_left), :] = folded(tbuf[:, pl.ds(LANES, LANES)])
        at += gate_rows_left
        spread(at, nn(low_t[rank:], gcat[:, pl.ds(hid, hid)]))
        at += gate_rows_right
        hid_all = hidden[...]
        aflat[pl.ds(at, gate_rows_right), :] = folded(nn(hid_all.T, low8[...]))
        at += gate_rows_right
        low_hidden = nt(hid_all, dal[...]).astype(jnp.bfloat16).astype(jnp.float32)
        low_hidden = (low_hidden * gate_col).astype(jnp.bfloat16)
        spread(at, nn(low_hidden.T, g_all))
        for d in range(n):
            ashare[d, pl.ds(0, share), :] = aflat[pl.ds(d * share, share), :]
        for c in range(2):
            for x in range(2):
                for z in range(line):
                    ebuf[slot(c, x, z), pl.ds(0, ashare.shape[1]), :] = ashare[index_of(c, x, z)].astype(
                        jnp.bfloat16
                    )

    plan = [0, CHUNKS] + list(range(1, CHUNKS))
    for k in range(len(plan) + 2):
        if k < len(plan):
            if plan[k] < CHUNKS:
                compute_rows(plan[k])
            else:
                compute_adapters()
            start_a(plan[k])
        if 1 <= k <= len(plan):
            stage_b(plan[k - 1])
        if k >= 2:
            stage_c(plan[k - 2])

    for i in range(CHUNKS):
        out_in[:, pl.ds(i * step, step)] = total(i).astype(jnp.bfloat16)
    extra = total(CHUNKS)
    out_adapt[...] = extra[:share]
    w_rows = extra[ebuf.shape[1] - t :]
    lanes_k = lax.broadcasted_iota(jnp.int32, (t, top), 1)
    picked = jnp.zeros((t, top), jnp.float32)
    for k in range(top):
        value = jnp.sum(jnp.where(lanes_t == chosen[:, k : k + 1], w_rows, 0.0), axis=1, keepdims=True)
        picked = picked + jnp.where(lanes_k == k, value, 0.0)
    out_comb[...] = picked.T
    for copy in sent:
        copy.wait_send()


def dense_shards(*operands):
    grad, tok, routes, combine, gate, upper, down, gal, gar, ual, uar, dal, dar = operands
    n = lax.axis_size("exp")
    line = n // 4
    t, width = tok.shape
    top, hid, rank = routes.shape[1], gate.shape[2], gar.shape[0]
    rep = LANES // rank
    params = 3 * rank * (width + hid)
    share = params // n // LANES
    padded = -(-share // 16) * 16
    rows, half, quarter = n * t, n // 2, n // 4
    step = width // CHUNKS
    extra = padded + t
    bf, f32 = jnp.bfloat16, jnp.float32
    scratch = [
        pltpu.VMEM((n, t, width), bf),
        pltpu.VMEM((n, t, width + LANES), bf),
        pltpu.VMEM((top, t), jnp.int32),
        pltpu.VMEM((width, 2 * hid), bf),
        pltpu.VMEM((hid, width), bf),
        pltpu.VMEM((2 * rank, width), bf),
        pltpu.VMEM((2 * rank, 2 * hid), bf),
        pltpu.VMEM((LANES, hid), bf),
        pltpu.VMEM((LANES, hid), bf),
        pltpu.VMEM((rank, hid), bf),
        pltpu.VMEM((LANES, width), bf),
        pltpu.VMEM((rows, hid), f32),
        pltpu.VMEM((rows, hid), f32),
        pltpu.VMEM((rows, hid), f32),
        pltpu.VMEM((rows, LANES), bf),
        pltpu.VMEM((width, rows), bf),
        pltpu.VMEM((rows, hid), bf),
        pltpu.VMEM((rows, 2 * hid), bf),
        pltpu.VMEM((rows, LANES), f32),
        pltpu.VMEM((width, 2 * LANES), f32),
        pltpu.VMEM((share * n, LANES), f32),
        pltpu.VMEM((n, padded, LANES), f32),
        pltpu.VMEM((CHUNKS, n, t, step), bf),
        pltpu.VMEM((CHUNKS, half, t, step), bf),
        pltpu.VMEM((CHUNKS, quarter, t, step), bf),
        pltpu.VMEM((CHUNKS, line - 1, t, step), bf),
        pltpu.VMEM((n, extra, LANES), bf),
        pltpu.VMEM((half, extra, LANES), bf),
        pltpu.VMEM((quarter, extra, LANES), bf),
        pltpu.VMEM((line - 1, extra, LANES), bf),
        pltpu.SemaphoreType.DMA((11 + 3 * rep,)),
        pltpu.SemaphoreType.DMA((PARTS, n)),
        pltpu.SemaphoreType.DMA((PARTS, n)),
        pltpu.SemaphoreType.DMA((PARTS, n)),
        pltpu.SemaphoreType.DMA((PARTS, n)),
        pltpu.SemaphoreType.DMA((CHUNKS + 1,)),
        pltpu.SemaphoreType.DMA((CHUNKS + 1,)),
        pltpu.SemaphoreType.DMA((CHUNKS + 1,)),
        pltpu.SemaphoreType.DMA((CHUNKS + 1,)),
        pltpu.SemaphoreType.DMA((CHUNKS + 1, line - 1)),
        pltpu.SemaphoreType.DMA((CHUNKS + 1, line - 1)),
    ]
    grad_in, grad_combine, adapters = pl.pallas_call(
        functools.partial(dense_kernel, n, line),
        out_shape=(
            jax.ShapeDtypeStruct((t, width), bf),
            jax.ShapeDtypeStruct((top, t), f32),
            jax.ShapeDtypeStruct((share, LANES), f32),
        ),
        in_specs=[pl.BlockSpec(memory_space=pltpu.VMEM if i == 3 else pl.ANY) for i in range(13)],
        out_specs=(pl.BlockSpec(memory_space=pltpu.VMEM),) * 3,
        scratch_shapes=scratch,
        compiler_params=pltpu.CompilerParams(
            collective_id=0, has_side_effects=True, vmem_limit_bytes=62 * 1024 * 1024
        ),
    )(grad, tok, routes.T, combine.T, gate, upper, down, gal.T, gar, ual.T, uar, dal.T, dar)
    return grad_in, grad_combine.astype(bf).T, adapters.reshape(-1)


def dense_fits(tokens, routes, gate, rank, groups, n):
    t, width = tokens.shape[0] // (groups * n), tokens.shape[1]
    top, hid = routes.shape[1], gate.shape[2]
    capacity = max(2, min(t, (2 * t * top + n - 1) // n))
    params = 3 * rank * (width + hid)
    return (
        capacity == t
        and t == 16
        and n % 4 == 0
        and 8 <= n <= LANES
        and gate.shape[0] == n
        and rank == 16
        and width % (CHUNKS * LANES) == 0
        and hid % LANES == 0
        and params % (n * LANES) == 0
    )


def solution(mesh):
    placed = (
        P(("grp", "exp"), None),
        P(("grp", "exp"), None),
        P(("grp", "exp"), None),
        P(("grp", "exp"), None),
        P("exp", None, None),
        P("exp", None, None),
        P("exp", None, None),
        P(),
        P(),
        P(),
        P(),
        P(),
        P(),
    )
    groups, n = mesh.shape["grp"], mesh.shape["exp"]

    def whole(*arrays):
        dense = dense_fits(arrays[1], arrays[2], arrays[4], arrays[8].shape[0], groups, n)
        return jax.shard_map(
            dense_shards if dense else shards,
            mesh=mesh,
            in_specs=placed,
            out_specs=(P(("grp", "exp"), None), P(("grp", "exp"), None), P(("grp", "exp"))),
            check_vma=False,
        )(*arrays)

    return whole
```
